32 devices in a mesh: parts: 2 (over y), tp: 4 (over z), section: 4 (over x, core).
Axes of the slice: x: 2, y: 2, z: 4, core: 2. Of those that a mesh axis runs over, the one named last changes fastest.
Arguments:
- memory: bfloat16 [8, 1024, 8192], P('parts', 'tp'), parts along dimension 0, may hold values from -6 to 6
- mem_lengths: int32 [8], P('parts'), parts along dimension 0, may hold values from 128 to 1024, as said below
- decode_group: int32 [8], P('parts'), parts along dimension 0, may hold values from 0 to 3, as said below
- row_counts: int32 [8], P('parts'), parts along dimension 0, may hold values from 1 to 32, as said below
- hidden: bfloat16 [16, 32, 8192], P(('parts', 'section')), parts along dimension 0, may hold values from -6 to 6
- norm_gain: bfloat16 [8192], replicated, may hold values from 0.5 to 1.5
- q_weight: bfloat16 [8192, 8192], P('section', 'tp'), may hold values from -0.0625 to 0.0625
- k_weight: bfloat16 [8192, 1024], P('tp', 'section'), may hold values from -0.0625 to 0.0625
- v_weight: bfloat16 [8192, 1024], P('tp', 'section'), may hold values from -0.0625 to 0.0625
- q_gain: float32 [128], replicated, may hold values from 0.5 to 1.5
- k_gain: float32 [128], replicated, may hold values from 0.5 to 1.5
- o_weight: bfloat16 [8192, 8192], P('tp', 'section'), may hold values from -0.25 to 0.25
Outputs:
- updated: bfloat16 [16, 32, 8192], P(('parts', 'section')), parts along dimension 0
The draws below stay inside these ranges and needn't reach their ends.
There are 2 independent parts, one for each index of `parts`. The reference program is written for one: setup_inputs(seed, part) draws one part's arguments, and reference() takes and returns one part's arrays. A program takes and returns all parts, laid end to end along the dimension named above; an argument that names none is the same for every part. Nothing has to cross between parts.
Inputs may be any that keep to these rules, and one draw needn't show every extreme that they name: `decode_group`: each group is named by at most 2 requests, and some group by exactly 2. `mem_lengths`: multiples of 128; some request has exactly 128 and another exactly 1024. `row_counts`: some request has exactly 32.
All inputs are finite; a program needn't handle non-finite values.
Results may differ from the reference program's by a relative error of at most 0.005.
Values may be sent and summed in bfloat16 or wider, within the bound.
A program may use at most 320 MiB of HBM per device.

```python
import jax
import jax.numpy as jnp
from jax import lax

D = 8192
KVH = 8
HD = 128
REQS = 4
MEM_LEN = 1024
ROWS = 32
CAP = 2
STEPS = 2
QW = 8192
KW = 1024
GROUP = 8
SLOTS = 8
N_SECTION = 4


def draw_decode_group(key, part):
    key = jax.random.fold_in(key, 11)
    first_key, other_key, perm_key = jax.random.split(key, 3)
    shared = jax.random.randint(first_key, (1,), 0, N_SECTION)
    others = (shared + jax.random.randint(other_key, (REQS - 2,), 1, N_SECTION)) % N_SECTION
    groups = jnp.concatenate([shared, shared, others]).astype(jnp.int32)
    return groups[jax.random.permutation(perm_key, REQS)]


def draw_mem_lengths(key, part):
    key = jax.random.fold_in(key, 12)
    value_key, index_key, short_key = jax.random.split(key, 3)
    blocks = jax.random.randint(value_key, (REQS,), 1, MEM_LEN // 128 + 1) * 128
    longest = jax.random.randint(index_key, (), 0, REQS)
    shortest = (longest + jax.random.randint(short_key, (), 1, REQS)) % REQS
    ordinal = jnp.arange(REQS)
    blocks = jnp.where(ordinal == shortest, 128, blocks)
    return jnp.where(ordinal == longest, MEM_LEN, blocks).astype(jnp.int32)


def draw_row_counts(key, part):
    key = jax.random.fold_in(key, 13)
    value_key, index_key = jax.random.split(key, 2)
    counts = jax.random.randint(value_key, (REQS,), 1, ROWS + 1)
    fullest = jax.random.randint(index_key, (), 0, REQS)
    return jnp.where(jnp.arange(REQS) == fullest, ROWS, counts).astype(jnp.int32)


def shard_levels(stream_key, shape, cuts, smallest, largest):
    level, own = 1.0, jax.random.fold_in(stream_key, 6)
    for axis_at, shards_of in cuts:
        steps = jnp.exp(jax.random.uniform(jax.random.fold_in(own, axis_at), (shards_of,), jnp.float32, smallest / len(cuts), largest / len(cuts)))
        level = level * jnp.repeat(steps, shape[axis_at] // shards_of).reshape([-1 if axis == axis_at else 1 for axis in range(len(shape))])
    return level


def gaussian(key, shape, scale, most, cuts=(), kind=jnp.bfloat16):
    level = shard_levels(key, shape, cuts, -0.22, 0.18) if cuts else 1.0
    values = jax.random.normal(key, shape, jnp.float32) * scale * level
    return jnp.minimum(jnp.maximum(values, -most), most).astype(kind)


def setup_inputs(seed: int = 0, part: int = 0) -> dict:
    streams_of = jax.random.split(jax.random.key(seed), 13)
    own_keys = jax.random.split(jax.random.fold_in(streams_of[12], part), 13)
    memory = gaussian(own_keys[0], (REQS, MEM_LEN, D), 1.0, 6.0, ((1, 4),))
    mem_lengths = draw_mem_lengths(jax.random.fold_in(jax.random.fold_in(streams_of[12], part), 71), part)
    decode_group = draw_decode_group(jax.random.fold_in(jax.random.fold_in(streams_of[12], part), 71), part)
    row_counts = draw_row_counts(jax.random.fold_in(jax.random.fold_in(streams_of[12], part), 71), part)
    hidden = gaussian(own_keys[4], (SLOTS, ROWS, D), 1.0, 6.0, ((0, 4),))
    norm_gain = jnp.clip(1.0 + 0.1 * jax.random.normal(streams_of[5], (D,), jnp.float32), 0.5, 1.5).astype(jnp.bfloat16)
    q_weight = gaussian(streams_of[6], (D, QW), D ** -0.5, 0.0625, ((0, 4), (1, 4)))
    k_weight = gaussian(streams_of[7], (D, KW), D ** -0.5, 0.0625, ((0, 4), (1, 4)))
    v_weight = gaussian(streams_of[8], (D, KW), D ** -0.5, 0.0625, ((0, 4), (1, 4)))
    q_gain = jnp.clip(1.0 + 0.1 * jax.random.normal(streams_of[9], (HD,), jnp.float32), 0.5, 1.5)
    k_gain = jnp.clip(1.0 + 0.1 * jax.random.normal(streams_of[10], (HD,), jnp.float32), 0.5, 1.5)
    o_weight = gaussian(streams_of[11], (QW, D), (QW // 16) ** -0.5, 0.25, ((0, 4), (1, 4)))
    return dict(memory=memory, mem_lengths=mem_lengths, decode_group=decode_group, row_counts=row_counts, hidden=hidden, norm_gain=norm_gain, q_weight=q_weight, k_weight=k_weight, v_weight=v_weight, q_gain=q_gain, k_gain=k_gain, o_weight=o_weight)


EPSILON = 1e-06

def head_norm(values_in, gain_vector):
    return values_in * lax.rsqrt(lax.optimization_barrier(jnp.mean(values_in * values_in, axis=-1, keepdims=True)) + EPSILON) * gain_vector

def slot_onehot(decode_group, groups, capacity):
    total = decode_group.shape[0]
    ordinal = jnp.arange(total, dtype=jnp.int32)
    matches = decode_group[None, :] == decode_group[:, None]
    slot_rank = lax.optimization_barrier(jnp.sum((matches & (ordinal[None, :] < ordinal[:, None])).astype(jnp.int32), axis=1))
    group_ids = jnp.arange(groups, dtype=jnp.int32)
    slot_ids = jnp.arange(capacity, dtype=jnp.int32)
    chosen = (decode_group[None, None, :] == group_ids[:, None, None]) & (slot_rank[None, None, :] == slot_ids[None, :, None])
    return chosen.astype(jnp.float32)

def reference(memory, mem_lengths, decode_group, row_counts, hidden, norm_gain, q_weight, k_weight, v_weight, q_gain, k_gain, o_weight):
    req_count, mem_len, model_width = memory.shape
    mem_rows = memory.reshape(req_count * mem_len, model_width)
    key_heads = head_norm(jnp.dot(mem_rows, k_weight, preferred_element_type=jnp.float32).reshape(req_count, mem_len, KVH, HD), k_gain).astype(jnp.bfloat16)
    value_heads = jnp.dot(mem_rows, v_weight, preferred_element_type=jnp.float32).reshape(req_count, mem_len, KVH, HD).astype(jnp.bfloat16)
    slot_map = slot_onehot(decode_group, N_SECTION, CAP).reshape(SLOTS, req_count)
    slot_keys = jnp.einsum('sr,rlkd->slkd', slot_map, key_heads.astype(jnp.float32))
    slot_values = jnp.einsum('sr,rlkd->slkd', slot_map, value_heads.astype(jnp.float32))
    occupied = lax.optimization_barrier(jnp.sum(slot_map, axis=1))
    key_len = lax.optimization_barrier(jnp.sum(slot_map * mem_lengths.astype(jnp.float32)[None, :], axis=1)) + (1.0 - occupied) * mem_len
    live_count = lax.optimization_barrier(jnp.sum(slot_map * row_counts.astype(jnp.float32)[None, :], axis=1))
    positions = jnp.arange(mem_len, dtype=jnp.float32)
    key_mask = (positions[None, :] < key_len[:, None]).astype(jnp.float32)
    row_live = (jnp.arange(ROWS, dtype=jnp.float32)[None, :] < live_count[:, None]).astype(jnp.float32)
    state = hidden
    for step_index in range(STEPS):
        state_f32 = state.astype(jnp.float32)
        normed = (state_f32 * lax.rsqrt(lax.optimization_barrier(jnp.mean(state_f32 * state_f32, axis=-1, keepdims=True)) + EPSILON) * norm_gain.astype(jnp.float32)).astype(jnp.bfloat16)
        queries = jnp.dot(normed.reshape(SLOTS * ROWS, model_width), q_weight, preferred_element_type=jnp.float32).reshape(SLOTS, ROWS, KVH, GROUP, HD)
        queries = (head_norm(queries, q_gain) * HD ** (-0.5)).astype(jnp.bfloat16)
        scores = jnp.einsum('srkgd,slkd->srkgl', queries.astype(jnp.float32), slot_keys)
        raw = jnp.exp(scores) * key_mask[:, None, None, None, :]
        softmax = (raw / lax.optimization_barrier(jnp.sum(raw, axis=-1, keepdims=True))).astype(jnp.bfloat16)
        attended = jnp.einsum('srkgl,slkd->srkgd', softmax.astype(jnp.float32), slot_values).astype(jnp.bfloat16).reshape(SLOTS * ROWS, QW)
        output = jnp.dot(attended, o_weight, preferred_element_type=jnp.float32)
        state = (state_f32 + row_live[:, :, None] * output.reshape(SLOTS, ROWS, model_width)).astype(jnp.bfloat16)
    return state
```

```python
import functools

import jax
import jax.numpy as jnp
from jax import lax
from jax.experimental import pallas as pl
from jax.experimental.pallas import tpu as pltpu
from jax.sharding import PartitionSpec as P

KVH = 8
HD = 128
STEPS = 2
GROUP = 8


EPSILON = 1e-06
MESH = pl.DeviceIdType.MESH
TILE = 512
VMEM_LIMIT = 58 * 1024 * 1024


def head_norm(values_in, gain_vector):
    return (
        values_in
        * lax.rsqrt(jnp.mean(values_in * values_in, axis=-1, keepdims=True) + EPSILON)
        * gain_vector
    )


def slot_onehot(decode_group, groups, capacity):
    total = decode_group.shape[0]
    ordinal = jnp.arange(total, dtype=jnp.int32)
    matches = decode_group[None, :] == decode_group[:, None]
    slot_rank = jnp.sum((matches & (ordinal[None, :] < ordinal[:, None])).astype(jnp.int32), axis=1)
    group_ids = jnp.arange(groups, dtype=jnp.int32)
    slot_ids = jnp.arange(capacity, dtype=jnp.int32)
    chosen = (decode_group[None, None, :] == group_ids[:, None, None]) & (
        slot_rank[None, None, :] == slot_ids[None, :, None]
    )
    return chosen.astype(jnp.float32)


def decode_kernel(
    n,
    lens_ref,
    rows_ref,
    map_ref,
    hidden_ref,
    gain_ref,
    qgain_ref,
    keys_ref,
    values_ref,
    qw_hbm,
    ow_hbm,
    out_ref,
    qw,
    ow,
    xs,
    hb,
    st,
    sq,
    rq,
    sn,
    rn,
    qn,
    aq,
    so,
    ro,
    sl,
    rl,
    at,
    aa,
    sb,
    rb,
    ob,
    rob,
    wsem,
    hsem,
    qsem,
    nsem,
    asem,
    osem,
    lsem,
    gsem,
    bsem,
    ssem,
    fsem,
):
    part = lax.axis_index("parts")
    t = lax.axis_index("tp")
    s = lax.axis_index("section")
    cap, rows, width = hidden_ref.shape
    block = width // n
    toks = keys_ref.shape[1]
    kv = keys_ref.shape[2] // HD
    diag = s == t
    sends = []

    def remote(src, dst, sems, i_send, i_recv, tp, section):
        return pltpu.make_async_remote_copy(
            src_ref=src,
            dst_ref=dst,
            send_sem=sems.at[0].at[i_send],
            recv_sem=sems.at[1].at[i_recv],
            device_id=(part, tp, section),
            device_id_type=MESH,
        )

    def send(*args):
        copy = remote(*args)
        copy.start()
        sends.append((copy, None))

    def send_or_keep(src, dst, *args):
        copy = remote(src, dst, *args)

        @pl.when(diag)
        def _():
            dst[...] = src[...]

        @pl.when(jnp.logical_not(diag))
        def _():
            copy.start()

        sends.append((copy, jnp.logical_not(diag)))

    def receive(dst, sems, i):
        remote(dst, dst, sems, i, i, t, s).wait_recv()

    def receive_or_kept(dst, sems, i):
        @pl.when(jnp.logical_not(diag))
        def _():
            receive(dst, sems, i)

    def ring(me, d):
        return lax.rem(me + d, n)

    qcopy = pltpu.make_async_copy(qw_hbm, qw, wsem.at[0])
    qcopy.start()
    ocopy = pltpu.make_async_copy(ow_hbm, ow, wsem.at[1])
    ocopy.start()

    barrier = pltpu.get_barrier_semaphore()
    for dt in range(n):
        for ds in range(n):
            if dt or ds:
                pl.semaphore_signal(
                    barrier, inc=1, device_id=(part, ring(t, dt), ring(s, ds)), device_id_type=MESH
                )
    pl.semaphore_wait(barrier, n * n - 1)

    def columns(i):
        return pl.ds(pl.multiple_of(i * block, block), block)

    for d in range(1, n):
        g = ring(s, d)
        send(hidden_ref.at[:, :, columns(g)], hb.at[s], hsem, g, s, t, g)
    hb[s] = hidden_ref[:, :, columns(s)]
    for d in range(1, n):
        g = ring(s, d)
        receive(hb.at[g], hsem, g)
    for r in range(n):
        held = jnp.zeros((rows, block), jnp.float32)
        for g in range(n):
            for c in range(cap):
                chosen = map_ref[g, c * n + r] > 0
                held = jnp.where(chosen, hb[g, c].astype(jnp.float32), held)
        st[0, r] = held.astype(jnp.bfloat16)

    for step in range(STEPS):
        state = st[step].reshape(n * rows, block).astype(jnp.float32)
        xs[...] = (state * gain_ref[...]).astype(jnp.bfloat16)
        squares = jnp.sum(state * state, axis=-1, keepdims=True)
        sn[step] = jnp.broadcast_to(squares, (n * rows, HD)).reshape(n, rows, HD)
        for d in range(1, n):
            g = ring(s, d)
            send(sn.at[step].at[g], rn.at[step].at[s], nsem.at[step], g, s, t, g)
        if step == 0:
            qcopy.wait()

        @pl.loop(0, block // TILE)
        def _(j):
            at_cols = pl.ds(pl.multiple_of(j * TILE, TILE), TILE)
            acc = jnp.dot(xs[...], qw[:, at_cols], preferred_element_type=jnp.float32)
            sq[step, :, :, at_cols] = acc.astype(jnp.bfloat16).reshape(n, rows, TILE)

        for d in range(1, n):
            g = ring(s, d)
            send(sq.at[step].at[g], rq.at[step].at[s], qsem.at[step], g, s, t, g)
        total = sq[step, s].astype(jnp.float32)
        norms = sn[step, s]
        for d in range(1, n):
            g = ring(s, d)
            receive(rn.at[step].at[g], nsem.at[step], g)
            receive(rq.at[step].at[g], qsem.at[step], g)
            total += rq[step, g].astype(jnp.float32)
            norms += rn[step, g]
        scale = lax.rsqrt(norms[:, :1] * (1.0 / width) + EPSILON)
        for h in range(block // HD):
            head = total[:, h * HD : (h + 1) * HD] * scale
            mean = jnp.mean(head * head, axis=-1, keepdims=True)
            qn[step, :, h * HD : (h + 1) * HD] = (
                head * lax.rsqrt(mean + EPSILON) * qgain_ref[...]
            ).astype(jnp.bfloat16)
        for d in range(1, n):
            send(qn.at[step], aq.at[step].at[s], asem.at[step], d, s, ring(t, d), t)
        send_or_keep(qn.at[step], aq.at[step].at[s], asem.at[step], 0, s, t, t)

        position = t * toks + lax.broadcasted_iota(jnp.int32, (1, toks), 1)
        lane = lax.broadcasted_iota(jnp.int32, (rows, HD), 1)
        for d in (1, 2, 3, 0) if n == 4 else range(n - 1, -1, -1):
            r = ring(s, d)
            if d:
                receive(aq.at[step].at[r], asem.at[step], r)
            else:
                receive_or_kept(aq.at[step].at[r], asem.at[step], r)
            live = position < lens_ref[r]
            sums = jnp.zeros((rows, HD), jnp.float32)
            for j in range(kv):
                cols = slice(j * HD, (j + 1) * HD)
                heads = [
                    aq[step, r, :, (j * GROUP + g) * HD : (j * GROUP + g + 1) * HD]
                    for g in range(GROUP)
                ]
                scores = lax.dot_general(
                    jnp.concatenate(heads, axis=0),
                    keys_ref[r, :, cols],
                    (((1,), (1,)), ((), ())),
                    preferred_element_type=jnp.float32,
                )
                raw = jnp.where(live, jnp.exp(scores), 0.0)
                total_raw = jnp.sum(raw, axis=-1, keepdims=True)
                mixed = jnp.dot(
                    raw.astype(jnp.bfloat16),
                    values_ref[r, :, cols],
                    preferred_element_type=jnp.float32,
                ).astype(jnp.bfloat16)
                for g in range(GROUP):
                    h = j * GROUP + g
                    span = slice(g * rows, (g + 1) * rows)
                    so[step, r, :, h * HD : (h + 1) * HD] = mixed[span]
                    sums = jnp.where(lane == h, total_raw[span], sums)
            sl[step, r] = sums
            put = send if d else send_or_keep
            put(sl.at[step].at[r], rl.at[step].at[t], lsem.at[step], d, t, s, r)
            put(so.at[step].at[r], ro.at[step].at[t], osem.at[step], d, t, s, r)
        for d in (1, 2, 3, 0) if n == 4 else range(n - 1, -1, -1):
            i = ring(t, d)
            get = receive if d else receive_or_kept
            get(rl.at[step].at[i], lsem.at[step], i)
            get(ro.at[step].at[i], osem.at[step], i)
        sums = rl[step, 0]
        for i in range(1, n):
            sums += rl[step, i]
        for h in range(block // HD):
            cols = slice(h * HD, (h + 1) * HD)
            mixed = ro[step, 0, :, cols].astype(jnp.float32)
            for i in range(1, n):
                mixed += ro[step, i, :, cols].astype(jnp.float32)
            at[step, :, cols] = (mixed / sums[:, h : h + 1]).astype(jnp.bfloat16)
        for d in range(1, n):
            g = ring(s, d)
            send(at.at[step], aa.at[step].at[s], gsem.at[step], g, s, t, g)
        aa[step, s] = at[step]
        if step == 0:
            ocopy.wait()
        for d in range(1, n):
            g = ring(s, d)
            receive(aa.at[step].at[g], gsem.at[step], g)

        @pl.loop(0, block // TILE)
        def _(j):
            at_cols = pl.ds(pl.multiple_of(j * TILE, TILE), TILE)
            acc = jnp.dot(
                aa[step].reshape(n * rows, block), ow[:, at_cols], preferred_element_type=jnp.float32
            )
            sb[step, :, :, at_cols] = acc.astype(jnp.bfloat16).reshape(n, rows, TILE)

        for d in (2, 1, 3) if n == 4 else range(1, n):
            i = ring(t, d)
            send(sb.at[step].at[i], rb.at[step].at[t], bsem.at[step], i, t, i, s)
        branch = sb[step, t].astype(jnp.float32)
        for d in range(1, n):
            i = ring(t, d)
            receive(rb.at[step].at[i], bsem.at[step], i)
            branch += rb[step, i].astype(jnp.float32)
        live_row = lax.broadcasted_iota(jnp.int32, (rows, 1), 0) < rows_ref[t]
        old = st[step, t].astype(jnp.float32)
        st[step + 1, t] = (old + jnp.where(live_row, branch, 0.0)).astype(jnp.bfloat16)
        for d in range(1, n):
            i = ring(t, d)
            send(st.at[step + 1].at[t], st.at[step + 1].at[t], ssem.at[step], i, t, i, s)
        for d in range(1, n):
            i = ring(t, d)
            receive(st.at[step + 1].at[i], ssem.at[step], i)

    for d in (1, 2, 3, 0) if n == 4 else range(n - 1, -1, -1):
        g = ring(s, d)
        for c in range(cap):
            held = jnp.zeros((rows, block), jnp.float32)
            for r in range(n):
                chosen = map_ref[g, c * n + r] > 0
                held = jnp.where(chosen, st[STEPS, r].astype(jnp.float32), held)
            ob[g, c] = held.astype(jnp.bfloat16)
        if d:
            send(ob.at[g], rob.at[s], fsem, g, s, t, g)
    rob[s] = ob[s]
    for d in range(1, n):
        g = ring(s, d)
        receive(rob.at[g], fsem, g)
    for c in range(cap):
        occupied = map_ref[s, c * n] + map_ref[s, c * n + 1]
        for r in range(2, n):
            occupied += map_ref[s, c * n + r]
        for g in range(n):
            cols = slice(g * block, (g + 1) * block)
            out_ref[c, :, cols] = jnp.where(
                occupied > 0,
                rob[g, c].astype(jnp.float32),
                hidden_ref[c, :, cols].astype(jnp.float32),
            ).astype(jnp.bfloat16)
    for copy, when in sends:
        if when is None:
            copy.wait_send()
        else:
            pl.when(when)(copy.wait_send)


def decode(n, lens, row_counts, slot_map, hidden, gain, q_gain, keys, values, q_weight, o_weight):
    cap, rows, width = hidden.shape
    block = width // n
    bf, f32 = jnp.bfloat16, jnp.float32
    vmem, smem = (pl.BlockSpec(memory_space=m) for m in (pltpu.VMEM, pltpu.SMEM))
    hbm = pl.BlockSpec(memory_space=pl.ANY)
    big, one = (STEPS, n, rows, block), (STEPS, rows, block)
    small = (STEPS, n, rows, HD)
    scratch = [
        pltpu.VMEM(q_weight.shape, bf),
        pltpu.VMEM(o_weight.shape, bf),
        pltpu.VMEM((n * rows, block), bf),
        pltpu.VMEM((n, cap, rows, block), bf),
        pltpu.VMEM((STEPS + 1, n, rows, block), bf),
        pltpu.VMEM(big, bf),
        pltpu.VMEM(big, bf),
        pltpu.VMEM(small, f32),
        pltpu.VMEM(small, f32),
        pltpu.VMEM(one, bf),
        pltpu.VMEM(big, bf),
        pltpu.VMEM(big, bf),
        pltpu.VMEM(big, bf),
        pltpu.VMEM(small, f32),
        pltpu.VMEM(small, f32),
        pltpu.VMEM(one, bf),
        pltpu.VMEM(big, bf),
        pltpu.VMEM(big, bf),
        pltpu.VMEM(big, bf),
        pltpu.VMEM((n, cap, rows, block), bf),
        pltpu.VMEM((n, cap, rows, block), bf),
        pltpu.SemaphoreType.DMA((2,)),
        pltpu.SemaphoreType.DMA((2, n)),
    ]
    scratch += [pltpu.SemaphoreType.DMA((STEPS, 2, n))] * 8
    scratch += [pltpu.SemaphoreType.DMA((2, n))]
    return pl.pallas_call(
        functools.partial(decode_kernel, n),
        out_shape=jax.ShapeDtypeStruct(hidden.shape, bf),
        in_specs=[smem] * 3 + [vmem] * 5 + [hbm] * 2,
        out_specs=vmem,
        scratch_shapes=scratch,
        compiler_params=pltpu.CompilerParams(
            collective_id=0, has_side_effects=True, vmem_limit_bytes=VMEM_LIMIT
        ),
        name="decode",
    )(lens, row_counts, slot_map, hidden, gain, q_gain, keys, values, q_weight, o_weight)


def square_body(
    memory,
    mem_lengths,
    decode_group,
    row_counts,
    hidden,
    norm_gain,
    q_weight,
    k_weight,
    v_weight,
    q_gain,
    k_gain,
    o_weight,
):
    n = lax.axis_size("tp")
    req_count, tok_local, model_width = memory.shape
    capacity = hidden.shape[0]
    mem_rows = memory.reshape(req_count * tok_local, model_width)
    key_acc = jnp.dot(
        mem_rows,
        lax.all_gather(k_weight, "tp", axis=0, tiled=True),
        preferred_element_type=jnp.float32,
    )
    value_acc = jnp.dot(
        mem_rows,
        lax.all_gather(v_weight, "tp", axis=0, tiled=True),
        preferred_element_type=jnp.float32,
    )
    keys = head_norm(key_acc.reshape(req_count, tok_local, -1, HD), k_gain)
    keys = keys.astype(jnp.bfloat16).reshape(req_count, tok_local, -1)
    values = value_acc.astype(jnp.bfloat16).reshape(req_count, tok_local, -1)
    slot_map = slot_onehot(decode_group, n, capacity).astype(jnp.int32)
    block = model_width // n
    gain = lax.dynamic_slice_in_dim(norm_gain, lax.axis_index("section") * block, block)
    return decode(
        n,
        mem_lengths,
        row_counts,
        slot_map.reshape(n, capacity * req_count),
        hidden,
        gain.astype(jnp.float32)[None, :],
        (q_gain * HD ** (-0.5))[None, :],
        keys,
        values,
        q_weight,
        o_weight,
    )


def body(
    memory,
    mem_lengths,
    decode_group,
    row_counts,
    hidden,
    norm_gain,
    q_weight,
    k_weight,
    v_weight,
    q_gain,
    k_gain,
    o_weight,
):
    tp_count = lax.axis_size("tp")
    section_count = lax.axis_size("section")
    req_count, tok_local, model_width = memory.shape
    capacity, row_count = (hidden.shape[0], hidden.shape[1])
    heads_local = q_weight.shape[1] // HD
    section_heads = k_weight.shape[1] // HD
    kv_local = max(1, heads_local // GROUP)
    per_kv = heads_local // kv_local
    mem_len = tok_local * tp_count
    mem_rows = memory.reshape(req_count * tok_local, model_width)
    key_acc = jnp.dot(
        mem_rows,
        lax.all_gather(k_weight, "tp", axis=0, tiled=True),
        preferred_element_type=jnp.float32,
    )
    value_acc = jnp.dot(
        mem_rows,
        lax.all_gather(v_weight, "tp", axis=0, tiled=True),
        preferred_element_type=jnp.float32,
    )
    key_heads = head_norm(key_acc.reshape(req_count, tok_local, section_heads, HD), k_gain).astype(
        jnp.bfloat16
    )
    value_heads = value_acc.reshape(req_count, tok_local, section_heads, HD).astype(jnp.bfloat16)
    packed = jnp.stack([key_heads, value_heads], axis=2)
    slot_map = slot_onehot(decode_group, section_count, capacity)
    outgoing = jnp.einsum(
        "gcr,rtvjd->gjctvd",
        slot_map.astype(jnp.bfloat16),
        packed,
        preferred_element_type=jnp.float32,
    ).astype(jnp.bfloat16)
    by_head = lax.all_to_all(outgoing, "section", split_axis=0, concat_axis=1, tiled=True)[0]
    repeat_count = tp_count * kv_local // KVH
    grouped = by_head.reshape(KVH // kv_local, kv_local, capacity, tok_local, 2, HD)
    spread = jnp.repeat(grouped, repeat_count, axis=0)
    mine = lax.all_to_all(spread, "tp", split_axis=0, concat_axis=3, tiled=True)[0]
    keys_mine = mine[:, :, :, 0, :]
    values_mine = mine[:, :, :, 1, :]
    q_full, o_full = (
        lax.all_gather(q_weight, "section", axis=0, tiled=True),
        lax.all_gather(o_weight, "section", axis=1, tiled=True),
    )
    group_index = lax.axis_index("section")
    my_slots = lax.dynamic_index_in_dim(slot_map, group_index, 0, keepdims=False)
    occupied = jnp.sum(my_slots, axis=1)
    key_len = (
        jnp.sum(my_slots * mem_lengths.astype(jnp.float32)[None, :], axis=1)
        + (1.0 - occupied) * mem_len
    )
    live_count = jnp.sum(my_slots * row_counts.astype(jnp.float32)[None, :], axis=1)
    key_mask = (jnp.arange(mem_len, dtype=jnp.float32)[None, :] < key_len[:, None]).astype(
        jnp.float32
    )
    row_live = (jnp.arange(row_count, dtype=jnp.float32)[None, :] < live_count[:, None]).astype(
        jnp.float32
    )
    state = hidden
    for step_index in range(STEPS):
        state_f32 = state.astype(jnp.float32)
        normed = (
            state_f32
            * lax.rsqrt(jnp.mean(state_f32 * state_f32, axis=-1, keepdims=True) + EPSILON)
            * norm_gain.astype(jnp.float32)
        ).astype(jnp.bfloat16)
        queries = jnp.dot(
            normed.reshape(capacity * row_count, model_width),
            q_full,
            preferred_element_type=jnp.float32,
        )
        queries = queries.reshape(capacity, row_count, kv_local, per_kv, HD)
        queries = (head_norm(queries, q_gain) * HD ** (-0.5)).astype(jnp.bfloat16)
        scores = jnp.einsum(
            "crkgd,kcld->crkgl", queries, keys_mine, preferred_element_type=jnp.float32
        )
        raw = jnp.exp(scores) * key_mask[:, None, None, None, :]
        softmax = (raw / jnp.sum(raw, axis=-1, keepdims=True)).astype(jnp.bfloat16)
        attended = jnp.einsum(
            "crkgl,kcld->crkgd", softmax, values_mine, preferred_element_type=jnp.float32
        )
        attended = attended.astype(jnp.bfloat16).reshape(capacity * row_count, heads_local * HD)
        branch = lax.psum(jnp.dot(attended, o_full, preferred_element_type=jnp.float32), "tp")
        state = (
            state_f32 + row_live[:, :, None] * branch.reshape(capacity, row_count, model_width)
        ).astype(jnp.bfloat16)
    return state


def solution(mesh):
    in_specs = (
        P("parts", "tp", None),
        P("parts"),
        P("parts"),
        P("parts"),
        P(("parts", "section"), None, None),
        P(),
        P("section", "tp"),
        P("tp", "section"),
        P("tp", "section"),
        P(),
        P(),
        P("tp", "section"),
    )
    out_specs = P(("parts", "section"), None, None)
    square = mesh.shape["tp"] == mesh.shape["section"]

    def whole(memory, *rest):
        requests = memory.shape[0] // mesh.shape["parts"]
        form = square_body if square and requests == mesh.shape["tp"] else body
        return jax.shard_map(
            form, mesh=mesh, in_specs=in_specs, out_specs=out_specs, check_vma=False
        )(memory, *rest)

    return whole
```

```python
import functools

import jax
import jax.numpy as jnp
from jax import lax
from jax.experimental import pallas as pl
from jax.experimental.pallas import tpu as pltpu
from jax.sharding import PartitionSpec as P

KVH = 8
HD = 128
STEPS = 2
GROUP = 8


EPSILON = 1e-06
MESH = pl.DeviceIdType.MESH
TILE = 512
VMEM_LIMIT = 60 * 1024 * 1024
SUB = 2
ROW_TILE = 256


def head_norm(values_in, gain_vector):
    return (
        values_in
        * lax.rsqrt(jnp.mean(values_in * values_in, axis=-1, keepdims=True) + EPSILON)
        * gain_vector
    )


def slot_onehot(decode_group, groups, capacity):
    total = decode_group.shape[0]
    ordinal = jnp.arange(total, dtype=jnp.int32)
    matches = decode_group[None, :] == decode_group[:, None]
    slot_rank = jnp.sum((matches & (ordinal[None, :] < ordinal[:, None])).astype(jnp.int32), axis=1)
    group_ids = jnp.arange(groups, dtype=jnp.int32)
    slot_ids = jnp.arange(capacity, dtype=jnp.int32)
    chosen = (decode_group[None, None, :] == group_ids[:, None, None]) & (
        slot_rank[None, None, :] == slot_ids[None, :, None]
    )
    return chosen.astype(jnp.float32)


def decode_kernel(
    n,
    lens_ref,
    rows_ref,
    map_ref,
    hidden_ref,
    gain_ref,
    qgain_ref,
    kgain_ref,
    mem_hbm,
    kw_hbm,
    vw_hbm,
    qw_hbm,
    ow_hbm,
    out_ref,
    mem,
    wkv,
    acc_kv,
    keys_ref,
    values_ref,
    qw,
    xs,
    hb,
    st,
    sq,
    rq,
    sn,
    rn,
    qn,
    aq,
    so,
    ro,
    sl,
    rl,
    at,
    aa,
    sb,
    rb,
    ob,
    rob,
    wsem,
    hsem,
    qsem,
    nsem,
    asem,
    osem,
    lsem,
    gsem,
    bsem,
    ssem,
    fsem,
    msem,
    lwsem,
    upsem,
    dnsem,
    zsem,
    ysem,
):
    part = lax.axis_index("parts")
    t = lax.axis_index("tp")
    s = lax.axis_index("section")
    cap, rows, width = hidden_ref.shape
    block = width // n
    toks = keys_ref.shape[1]
    kv = keys_ref.shape[2] // HD
    peer = 1 - part
    sub_rows = wkv.shape[4]
    half_block = mem.shape[2]
    diag = s == t
    sends = []

    def remote(src, dst, sems, i_send, i_recv, tp, section):
        return pltpu.make_async_remote_copy(
            src_ref=src,
            dst_ref=dst,
            send_sem=sems.at[0].at[i_send],
            recv_sem=sems.at[1].at[i_recv],
            device_id=(part, tp, section),
            device_id_type=MESH,
        )

    def send(*args):
        copy = remote(*args)
        copy.start()
        sends.append((copy, None))

    def send_or_keep(src, dst, *args):
        copy = remote(src, dst, *args)

        @pl.when(diag)
        def _():
            dst[...] = src[...]

        @pl.when(jnp.logical_not(diag))
        def _():
            copy.start()

        sends.append((copy, jnp.logical_not(diag)))

    def receive(dst, sems, i):
        remote(dst, dst, sems, i, i, t, s).wait_recv()

    def receive_or_kept(dst, sems, i):
        @pl.when(jnp.logical_not(diag))
        def _():
            receive(dst, sems, i)

    def ring(me, d):
        return lax.rem(me + d, n)

    qcopy = pltpu.make_async_copy(qw_hbm, qw, wsem.at[0])
    qcopy.start()

    barrier = pltpu.get_barrier_semaphore()
    for dt in range(n):
        for ds in range(n):
            if dt or ds:
                pl.semaphore_signal(
                    barrier, inc=1, device_id=(part, ring(t, dt), ring(s, ds)), device_id_type=MESH
                )
    pl.semaphore_signal(barrier, inc=1, device_id=(peer, t, s), device_id_type=MESH)
    pl.semaphore_wait(barrier, n * n)

    pieces = [(w, u) for w in range(2) for u in range(SUB)]

    def move(src, dst, send_sem, recv_sem, part_to, tp_to):
        return pltpu.make_async_remote_copy(
            src_ref=src,
            dst_ref=dst,
            send_sem=send_sem,
            recv_sem=recv_sem,
            device_id=(part_to, tp_to, s),
            device_id_type=MESH,
        )

    def start_if(copy, when):
        pl.when(when)(copy.start)
        sends.append((copy, when))

    above, below = t < n - 1, t > 0
    up, down = lax.rem(t + 1, n), lax.rem(t + n - 1, n)
    for c, (w, u) in enumerate(pieces):
        first = pl.multiple_of((part * SUB + u) * sub_rows, sub_rows)
        src = (kw_hbm, vw_hbm)[w].at[pl.ds(first, sub_rows), :]
        dst = wkv.at[t, w, part, u]
        start_if(move(src, dst, upsem.at[t, c], zsem.at[t, c], part, up), above)
        start_if(move(src, dst, dnsem.at[t, c], zsem.at[t, c], part, down), below)

    own_copies = [
        pltpu.make_async_copy(
            (kw_hbm, vw_hbm)[w].at[pl.ds((q * SUB + u) * sub_rows, sub_rows), :],
            wkv.at[t, w, q, u],
            lwsem.at[w, q, u],
        )
        for w in range(2)
        for q in range(2)
        for u in range(SUB)
    ]
    for copy in own_copies:
        copy.start()

    def mem_copies(i):
        return [
            pltpu.make_async_copy(
                mem_hbm.at[:, pl.ds(pl.multiple_of(i * block + k * half_block, half_block), half_block)],
                mem.at[2 * i + k],
                msem.at[i, k],
            )
            for k in range(2)
        ]

    for d in range(n):
        for copy in mem_copies(ring(t, d)):
            copy.start()

    def project(i, fresh):
        for copy in mem_copies(i):
            copy.wait()

        @pl.loop(0, mem.shape[1] // ROW_TILE)
        def _(j):
            at_rows = pl.ds(pl.multiple_of(j * ROW_TILE, ROW_TILE), ROW_TILE)
            for w in range(2):
                acc = jnp.zeros((ROW_TILE, kv * HD), jnp.float32) if fresh else acc_kv[w, at_rows, :]
                for k in range(2):
                    acc += jnp.dot(
                        mem[2 * i + k, at_rows, :],
                        wkv[i, w, k].reshape(half_block, kv * HD),
                        preferred_element_type=jnp.float32,
                    )
                acc_kv[w, at_rows, :] = acc

    def arrivals(d):
        yield ring(t, n - d), t - d >= 0, up, above, upsem
        yield ring(t, d), t + d < n, down, below, dnsem

    def relay(d):
        for c, (w, u) in enumerate(pieces):
            for i, here, onward, further, out_sem in arrivals(d):
                piece = wkv.at[i, w, part, u]

                @pl.when(here)
                def _():
                    move(piece, piece, out_sem.at[i, c], zsem.at[i, c], part, t).wait_recv()

                start_if(
                    move(piece, piece, out_sem.at[i, c], zsem.at[i, c], part, onward),
                    jnp.logical_and(here, further),
                )
                start_if(move(piece, piece, ysem.at[0, i, c], ysem.at[1, i, c], peer, t), here)

    def absorb(d):
        for i, here, _, _, _ in arrivals(d):

            @pl.when(here)
            def _():
                for c, (w, u) in enumerate(pieces):
                    piece = wkv.at[i, w, peer, u]
                    move(piece, piece, ysem.at[0, i, c], ysem.at[1, i, c], peer, t).wait_recv()
                project(i, False)

    def columns(i):
        return pl.ds(pl.multiple_of(i * block, block), block)

    for d in range(1, n):
        g = ring(s, d)
        send(hidden_ref.at[:, :, columns(g)], hb.at[s], hsem, g, s, t, g)
    hb[s] = hidden_ref[:, :, columns(s)]
    for copy in own_copies:
        copy.wait()
    project(t, True)
    for d in range(1, n):
        g = ring(s, d)
        receive(hb.at[g], hsem, g)
    for r in range(n):
        held = jnp.zeros((rows, block), jnp.float32)
        for g in range(n):
            for c in range(cap):
                chosen = map_ref[g, c * n + r] > 0
                held = jnp.where(chosen, hb[g, c].astype(jnp.float32), held)
        st[0, r] = held.astype(jnp.bfloat16)

    for step in range(STEPS):
        state = st[step].reshape(n * rows, block).astype(jnp.float32)
        xs[...] = (state * gain_ref[...]).astype(jnp.bfloat16)
        squares = jnp.sum(state * state, axis=-1, keepdims=True)
        sn[step] = jnp.broadcast_to(squares, (n * rows, HD)).reshape(n, rows, HD)
        for d in range(1, n):
            g = ring(s, d)
            send(sn.at[step].at[g], rn.at[step].at[s], nsem.at[step], g, s, t, g)
        if step == 0:
            qcopy.wait()

        @pl.loop(0, block // TILE)
        def _(j):
            at_cols = pl.ds(pl.multiple_of(j * TILE, TILE), TILE)
            acc = jnp.dot(xs[...], qw[:, at_cols], preferred_element_type=jnp.float32)
            sq[step, :, :, at_cols] = acc.astype(jnp.bfloat16).reshape(n, rows, TILE)

        for d in range(1, n):
            g = ring(s, d)
            send(sq.at[step].at[g], rq.at[step].at[s], qsem.at[step], g, s, t, g)
        if step == 0:
            relay(1)
        total = sq[step, s].astype(jnp.float32)
        norms = sn[step, s]
        for d in range(1, n):
            g = ring(s, d)
            receive(rn.at[step].at[g], nsem.at[step], g)
            receive(rq.at[step].at[g], qsem.at[step], g)
            total += rq[step, g].astype(jnp.float32)
            norms += rn[step, g]
        scale = lax.rsqrt(norms[:, :1] * (1.0 / width) + EPSILON)
        for h in range(block // HD):
            head = total[:, h * HD : (h + 1) * HD] * scale
            mean = jnp.mean(head * head, axis=-1, keepdims=True)
            qn[step, :, h * HD : (h + 1) * HD] = (
                head * lax.rsqrt(mean + EPSILON) * qgain_ref[...]
            ).astype(jnp.bfloat16)
        for d in range(1, n):
            send(qn.at[step], aq.at[step].at[s], asem.at[step], d, s, ring(t, d), t)
        send_or_keep(qn.at[step], aq.at[step].at[s], asem.at[step], 0, s, t, t)

        if step == 0:
            for d in range(2, n):
                absorb(d - 1)
                relay(d)
            absorb(n - 1)
            ocopies = [
                pltpu.make_async_copy(
                    ow_hbm.at[
                        pl.ds(k * half_block, half_block), pl.ds(c * half_block, half_block)
                    ],
                    mem.at[2 * k + c],
                    wsem.at[1 + 2 * k + c],
                )
                for c in range(2)
                for k in range(2)
            ]
            for copy in ocopies:
                copy.start()

            @pl.loop(0, n)
            def _(r):
                at_rows = pl.ds(pl.multiple_of(r * toks, toks), toks)
                for j in range(kv):
                    cols = slice(j * HD, (j + 1) * HD)
                    keys_ref[r, :, cols] = head_norm(acc_kv[0, at_rows, cols], kgain_ref[...]).astype(
                        jnp.bfloat16
                    )
                values_ref[r] = acc_kv[1, at_rows, :].astype(jnp.bfloat16)

        position = t * toks + lax.broadcasted_iota(jnp.int32, (1, toks), 1)
        lane = lax.broadcasted_iota(jnp.int32, (rows, HD), 1)
        for d in (1, 2, 3, 0) if n == 4 else range(n - 1, -1, -1):
            r = ring(s, d)
            if d:
                receive(aq.at[step].at[r], asem.at[step], r)
            else:
                receive_or_kept(aq.at[step].at[r], asem.at[step], r)
            live = position < lens_ref[r]
            sums = jnp.zeros((rows, HD), jnp.float32)
            for j in range(kv):
                cols = slice(j * HD, (j + 1) * HD)
                heads = [
                    aq[step, r, :, (j * GROUP + g) * HD : (j * GROUP + g + 1) * HD]
                    for g in range(GROUP)
                ]
                scores = lax.dot_general(
                    jnp.concatenate(heads, axis=0),
                    keys_ref[r, :, cols],
                    (((1,), (1,)), ((), ())),
                    preferred_element_type=jnp.float32,
                )
                raw = jnp.where(live, jnp.exp(scores), 0.0)
                total_raw = jnp.sum(raw, axis=-1, keepdims=True)
                mixed = jnp.dot(
                    raw.astype(jnp.bfloat16),
                    values_ref[r, :, cols],
                    preferred_element_type=jnp.float32,
                ).astype(jnp.bfloat16)
                for g in range(GROUP):
                    h = j * GROUP + g
                    span = slice(g * rows, (g + 1) * rows)
                    so[step, r, :, h * HD : (h + 1) * HD] = mixed[span]
                    sums = jnp.where(lane == h, total_raw[span], sums)
            sl[step, r] = sums
            put = send if d else send_or_keep
            put(sl.at[step].at[r], rl.at[step].at[t], lsem.at[step], d, t, s, r)
            put(so.at[step].at[r], ro.at[step].at[t], osem.at[step], d, t, s, r)
        for d in (1, 2, 3, 0) if n == 4 else range(n - 1, -1, -1):
            i = ring(t, d)
            get = receive if d else receive_or_kept
            get(rl.at[step].at[i], lsem.at[step], i)
            get(ro.at[step].at[i], osem.at[step], i)
        sums = rl[step, 0]
        for i in range(1, n):
            sums += rl[step, i]
        for h in range(block // HD):
            cols = slice(h * HD, (h + 1) * HD)
            mixed = ro[step, 0, :, cols].astype(jnp.float32)
            for i in range(1, n):
                mixed += ro[step, i, :, cols].astype(jnp.float32)
            at[step, :, cols] = (mixed / sums[:, h : h + 1]).astype(jnp.bfloat16)
        for d in range(1, n):
            g = ring(s, d)
            send(at.at[step], aa.at[step].at[s], gsem.at[step], g, s, t, g)
        aa[step, s] = at[step]
        if step == 0:
            for copy in ocopies:
                copy.wait()
        for d in range(1, n):
            g = ring(s, d)
            receive(aa.at[step].at[g], gsem.at[step], g)

        for c in range(2):

            @pl.loop(0, half_block // TILE)
            def _(j):
                in_cols = pl.ds(pl.multiple_of(j * TILE, TILE), TILE)
                at_cols = pl.ds(pl.multiple_of(c * half_block + j * TILE, TILE), TILE)
                mixed_rows = aa[step].reshape(n * rows, block)
                acc = jnp.dot(
                    mixed_rows[:, :half_block],
                    mem[c, :, in_cols],
                    preferred_element_type=jnp.float32,
                ) + jnp.dot(
                    mixed_rows[:, half_block:],
                    mem[2 + c, :, in_cols],
                    preferred_element_type=jnp.float32,
                )
                sb[step, :, :, at_cols] = acc.astype(jnp.bfloat16).reshape(n, rows, TILE)

        for d in (2, 1, 3) if n == 4 else range(1, n):
            i = ring(t, d)
            send(sb.at[step].at[i], rb.at[step].at[t], bsem.at[step], i, t, i, s)
        branch = sb[step, t].astype(jnp.float32)
        for d in range(1, n):
            i = ring(t, d)
            receive(rb.at[step].at[i], bsem.at[step], i)
            branch += rb[step, i].astype(jnp.float32)
        live_row = lax.broadcasted_iota(jnp.int32, (rows, 1), 0) < rows_ref[t]
        old = st[step, t].astype(jnp.float32)
        st[step + 1, t] = (old + jnp.where(live_row, branch, 0.0)).astype(jnp.bfloat16)
        for d in range(1, n):
            i = ring(t, d)
            send(st.at[step + 1].at[t], st.at[step + 1].at[t], ssem.at[step], i, t, i, s)
        for d in range(1, n):
            i = ring(t, d)
            receive(st.at[step + 1].at[i], ssem.at[step], i)

    for d in (1, 2, 3, 0) if n == 4 else range(n - 1, -1, -1):
        g = ring(s, d)
        for c in range(cap):
            held = jnp.zeros((rows, block), jnp.float32)
            for r in range(n):
                chosen = map_ref[g, c * n + r] > 0
                held = jnp.where(chosen, st[STEPS, r].astype(jnp.float32), held)
            ob[g, c] = held.astype(jnp.bfloat16)
        if d:
            send(ob.at[g], rob.at[s], fsem, g, s, t, g)
    rob[s] = ob[s]
    for d in range(1, n):
        g = ring(s, d)
        receive(rob.at[g], fsem, g)
    for c in range(cap):
        occupied = map_ref[s, c * n] + map_ref[s, c * n + 1]
        for r in range(2, n):
            occupied += map_ref[s, c * n + r]
        for g in range(n):
            cols = slice(g * block, (g + 1) * block)
            out_ref[c, :, cols] = jnp.where(
                occupied > 0,
                rob[g, c].astype(jnp.float32),
                hidden_ref[c, :, cols].astype(jnp.float32),
            ).astype(jnp.bfloat16)
    for copy, when in sends:
        if when is None:
            copy.wait_send()
        else:
            pl.when(when)(copy.wait_send)


def decode(
    n,
    lens,
    row_counts,
    slot_map,
    hidden,
    gain,
    q_gain,
    k_gain,
    mem_rows,
    k_weight,
    v_weight,
    q_weight,
    o_weight,
):
    cap, rows, width = hidden.shape
    block = width // n
    feats = k_weight.shape[1]
    bf, f32 = jnp.bfloat16, jnp.float32
    vmem, smem = (pl.BlockSpec(memory_space=m) for m in (pltpu.VMEM, pltpu.SMEM))
    hbm = pl.BlockSpec(memory_space=pl.ANY)
    big, one = (STEPS, n, rows, block), (STEPS, rows, block)
    small = (STEPS, n, rows, HD)
    scratch = [
        pltpu.VMEM((2 * n, mem_rows.shape[0], block // 2), bf),
        pltpu.VMEM((n, 2, 2, SUB, block // 2 // SUB, feats), bf),
        pltpu.VMEM((2, mem_rows.shape[0], feats), f32),
        pltpu.VMEM((n, mem_rows.shape[0] // n, feats), bf),
        pltpu.VMEM((n, mem_rows.shape[0] // n, feats), bf),
        pltpu.VMEM(q_weight.shape, bf),
        pltpu.VMEM((n * rows, block), bf),
        pltpu.VMEM((n, cap, rows, block), bf),
        pltpu.VMEM((STEPS + 1, n, rows, block), bf),
        pltpu.VMEM(big, bf),
        pltpu.VMEM(big, bf),
        pltpu.VMEM(small, f32),
        pltpu.VMEM(small, f32),
        pltpu.VMEM(one, bf),
        pltpu.VMEM(big, bf),
        pltpu.VMEM(big, bf),
        pltpu.VMEM(big, bf),
        pltpu.VMEM(small, f32),
        pltpu.VMEM(small, f32),
        pltpu.VMEM(one, bf),
        pltpu.VMEM(big, bf),
        pltpu.VMEM(big, bf),
        pltpu.VMEM(big, bf),
        pltpu.VMEM((n, cap, rows, block), bf),
        pltpu.VMEM((n, cap, rows, block), bf),
        pltpu.SemaphoreType.DMA((5,)),
        pltpu.SemaphoreType.DMA((2, n)),
    ]
    scratch += [pltpu.SemaphoreType.DMA((STEPS, 2, n))] * 8
    scratch += [
        pltpu.SemaphoreType.DMA((2, n)),
        pltpu.SemaphoreType.DMA((n, 2)),
        pltpu.SemaphoreType.DMA((2, 2, SUB)),
        pltpu.SemaphoreType.DMA((n, 2 * SUB)),
        pltpu.SemaphoreType.DMA((n, 2 * SUB)),
        pltpu.SemaphoreType.DMA((n, 2 * SUB)),
        pltpu.SemaphoreType.DMA((2, n, 2 * SUB)),
    ]
    return pl.pallas_call(
        functools.partial(decode_kernel, n),
        out_shape=jax.ShapeDtypeStruct(hidden.shape, bf),
        in_specs=[smem] * 3 + [vmem] * 4 + [hbm] * 5,
        out_specs=vmem,
        scratch_shapes=scratch,
        compiler_params=pltpu.CompilerParams(
            collective_id=0, has_side_effects=True, vmem_limit_bytes=VMEM_LIMIT
        ),
        name="decode",
    )(
        lens,
        row_counts,
        slot_map,
        hidden,
        gain,
        q_gain,
        k_gain,
        mem_rows,
        k_weight,
        v_weight,
        q_weight,
        o_weight,
    )


def square_body(
    memory,
    mem_lengths,
    decode_group,
    row_counts,
    hidden,
    norm_gain,
    q_weight,
    k_weight,
    v_weight,
    q_gain,
    k_gain,
    o_weight,
):
    n = lax.axis_size("tp")
    req_count, tok_local, model_width = memory.shape
    capacity = hidden.shape[0]
    mem_rows = memory.reshape(req_count * tok_local, model_width)
    slot_map = slot_onehot(decode_group, n, capacity).astype(jnp.int32)
    block = model_width // n
    gain = lax.dynamic_slice_in_dim(norm_gain, lax.axis_index("section") * block, block)
    return decode(
        n,
        mem_lengths,
        row_counts,
        slot_map.reshape(n, capacity * req_count),
        hidden,
        gain.astype(jnp.float32)[None, :],
        (q_gain * HD ** (-0.5))[None, :],
        k_gain[None, :],
        mem_rows,
        k_weight,
        v_weight,
        q_weight,
        o_weight,
    )


def body(
    memory,
    mem_lengths,
    decode_group,
    row_counts,
    hidden,
    norm_gain,
    q_weight,
    k_weight,
    v_weight,
    q_gain,
    k_gain,
    o_weight,
):
    tp_count = lax.axis_size("tp")
    section_count = lax.axis_size("section")
    req_count, tok_local, model_width = memory.shape
    capacity, row_count = (hidden.shape[0], hidden.shape[1])
    heads_local = q_weight.shape[1] // HD
    section_heads = k_weight.shape[1] // HD
    kv_local = max(1, heads_local // GROUP)
    per_kv = heads_local // kv_local
    mem_len = tok_local * tp_count
    mem_rows = memory.reshape(req_count * tok_local, model_width)
    key_acc = jnp.dot(
        mem_rows,
        lax.all_gather(k_weight, "tp", axis=0, tiled=True),
        preferred_element_type=jnp.float32,
    )
    value_acc = jnp.dot(
        mem_rows,
        lax.all_gather(v_weight, "tp", axis=0, tiled=True),
        preferred_element_type=jnp.float32,
    )
    key_heads = head_norm(key_acc.reshape(req_count, tok_local, section_heads, HD), k_gain).astype(
        jnp.bfloat16
    )
    value_heads = value_acc.reshape(req_count, tok_local, section_heads, HD).astype(jnp.bfloat16)
    packed = jnp.stack([key_heads, value_heads], axis=2)
    slot_map = slot_onehot(decode_group, section_count, capacity)
    outgoing = jnp.einsum(
        "gcr,rtvjd->gjctvd",
        slot_map.astype(jnp.bfloat16),
        packed,
        preferred_element_type=jnp.float32,
    ).astype(jnp.bfloat16)
    by_head = lax.all_to_all(outgoing, "section", split_axis=0, concat_axis=1, tiled=True)[0]
    repeat_count = tp_count * kv_local // KVH
    grouped = by_head.reshape(KVH // kv_local, kv_local, capacity, tok_local, 2, HD)
    spread = jnp.repeat(grouped, repeat_count, axis=0)
    mine = lax.all_to_all(spread, "tp", split_axis=0, concat_axis=3, tiled=True)[0]
    keys_mine = mine[:, :, :, 0, :]
    values_mine = mine[:, :, :, 1, :]
    q_full, o_full = (
        lax.all_gather(q_weight, "section", axis=0, tiled=True),
        lax.all_gather(o_weight, "section", axis=1, tiled=True),
    )
    group_index = lax.axis_index("section")
    my_slots = lax.dynamic_index_in_dim(slot_map, group_index, 0, keepdims=False)
    occupied = jnp.sum(my_slots, axis=1)
    key_len = (
        jnp.sum(my_slots * mem_lengths.astype(jnp.float32)[None, :], axis=1)
        + (1.0 - occupied) * mem_len
    )
    live_count = jnp.sum(my_slots * row_counts.astype(jnp.float32)[None, :], axis=1)
    key_mask = (jnp.arange(mem_len, dtype=jnp.float32)[None, :] < key_len[:, None]).astype(
        jnp.float32
    )
    row_live = (jnp.arange(row_count, dtype=jnp.float32)[None, :] < live_count[:, None]).astype(
        jnp.float32
    )
    state = hidden
    for step_index in range(STEPS):
        state_f32 = state.astype(jnp.float32)
        normed = (
            state_f32
            * lax.rsqrt(jnp.mean(state_f32 * state_f32, axis=-1, keepdims=True) + EPSILON)
            * norm_gain.astype(jnp.float32)
        ).astype(jnp.bfloat16)
        queries = jnp.dot(
            normed.reshape(capacity * row_count, model_width),
            q_full,
            preferred_element_type=jnp.float32,
        )
        queries = queries.reshape(capacity, row_count, kv_local, per_kv, HD)
        queries = (head_norm(queries, q_gain) * HD ** (-0.5)).astype(jnp.bfloat16)
        scores = jnp.einsum(
            "crkgd,kcld->crkgl", queries, keys_mine, preferred_element_type=jnp.float32
        )
        raw = jnp.exp(scores) * key_mask[:, None, None, None, :]
        softmax = (raw / jnp.sum(raw, axis=-1, keepdims=True)).astype(jnp.bfloat16)
        attended = jnp.einsum(
            "crkgl,kcld->crkgd", softmax, values_mine, preferred_element_type=jnp.float32
        )
        attended = attended.astype(jnp.bfloat16).reshape(capacity * row_count, heads_local * HD)
        branch = lax.psum(jnp.dot(attended, o_full, preferred_element_type=jnp.float32), "tp")
        state = (
            state_f32 + row_live[:, :, None] * branch.reshape(capacity, row_count, model_width)
        ).astype(jnp.bfloat16)
    return state


def solution(mesh):
    in_specs = (
        P("parts", "tp", None),
        P("parts"),
        P("parts"),
        P("parts"),
        P(("parts", "section"), None, None),
        P(),
        P("section", "tp"),
        P("tp", "section"),
        P("tp", "section"),
        P(),
        P(),
        P("tp", "section"),
    )
    out_specs = P(("parts", "section"), None, None)

    def whole(memory, *rest):
        parts, tp = mesh.shape["parts"], mesh.shape["tp"]
        requests, tokens, width = memory.shape
        square = parts == 2 and tp == mesh.shape["section"] and requests == parts * tp
        square = square and 2 * requests * tokens == parts * width
        form = square_body if square else body
        return jax.shard_map(
            form, mesh=mesh, in_specs=in_specs, out_specs=out_specs, check_vma=False
        )(memory, *rest)

    return whole
```

```python
import functools

import jax
import jax.numpy as jnp
from jax import lax
from jax.experimental import pallas as pl
from jax.experimental.pallas import tpu as pltpu
from jax.sharding import PartitionSpec as P

KVH = 8
HD = 128
STEPS = 2
GROUP = 8


EPSILON = 1e-06
MESH = pl.DeviceIdType.MESH
TILE = 512
VMEM_LIMIT = 60 * 1024 * 1024
SUB = 2
ROW_TILE = 256


def head_norm(values_in, gain_vector):
    return (
        values_in
        * lax.rsqrt(jnp.mean(values_in * values_in, axis=-1, keepdims=True) + EPSILON)
        * gain_vector
    )


def slot_onehot(decode_group, groups, capacity):
    total = decode_group.shape[0]
    ordinal = jnp.arange(total, dtype=jnp.int32)
    matches = decode_group[None, :] == decode_group[:, None]
    slot_rank = jnp.sum((matches & (ordinal[None, :] < ordinal[:, None])).astype(jnp.int32), axis=1)
    group_ids = jnp.arange(groups, dtype=jnp.int32)
    slot_ids = jnp.arange(capacity, dtype=jnp.int32)
    chosen = (decode_group[None, None, :] == group_ids[:, None, None]) & (
        slot_rank[None, None, :] == slot_ids[None, :, None]
    )
    return chosen.astype(jnp.float32)


def decode_kernel(
    n,
    lens_ref,
    rows_ref,
    map_ref,
    hidden_ref,
    gain_ref,
    qgain_ref,
    kgain_ref,
    mem_hbm,
    kw_hbm,
    vw_hbm,
    qw_hbm,
    ow_hbm,
    out_ref,
    mem,
    wkv,
    acc_kv,
    keys_ref,
    values_ref,
    qw,
    xs,
    hb,
    st,
    sq,
    rq,
    sn,
    rn,
    qn,
    aq,
    so,
    xo,
    ro,
    sl,
    xl,
    rl,
    at,
    aa,
    sb,
    rb,
    ob,
    rob,
    wsem,
    hsem,
    qsem,
    nsem,
    asem,
    xosem,
    xlsem,
    osem,
    lsem,
    gsem,
    bsem,
    ssem,
    fsem,
    msem,
    lwsem,
    upsem,
    dnsem,
    zsem,
    ysem,
):
    part = lax.axis_index("parts")
    t = lax.axis_index("tp")
    s = lax.axis_index("section")
    cap, rows, width = hidden_ref.shape
    block = width // n
    toks = keys_ref.shape[1]
    kv = keys_ref.shape[2] // HD
    peer = 1 - part
    sub_rows = wkv.shape[4]
    half_block = mem.shape[2]
    diag = s == t
    sends = []

    def remote(src, dst, sems, i_send, i_recv, tp, section):
        return pltpu.make_async_remote_copy(
            src_ref=src,
            dst_ref=dst,
            send_sem=sems.at[0].at[i_send],
            recv_sem=sems.at[1].at[i_recv],
            device_id=(part, tp, section),
            device_id_type=MESH,
        )

    def send(*args):
        copy = remote(*args)
        copy.start()
        sends.append((copy, None))

    def send_or_keep(src, dst, *args):
        copy = remote(src, dst, *args)

        @pl.when(diag)
        def _():
            dst[...] = src[...]

        @pl.when(jnp.logical_not(diag))
        def _():
            copy.start()

        sends.append((copy, jnp.logical_not(diag)))

    def receive(dst, sems, i):
        remote(dst, dst, sems, i, i, t, s).wait_recv()

    def receive_or_kept(dst, sems, i):
        @pl.when(jnp.logical_not(diag))
        def _():
            receive(dst, sems, i)

    def ring(me, d):
        return lax.rem(me + d, n)

    qcopy = pltpu.make_async_copy(qw_hbm, qw, wsem.at[0])
    qcopy.start()

    barrier = pltpu.get_barrier_semaphore()
    for dt in range(n):
        for ds in range(n):
            if dt or ds:
                pl.semaphore_signal(
                    barrier, inc=1, device_id=(part, ring(t, dt), ring(s, ds)), device_id_type=MESH
                )
    pl.semaphore_signal(barrier, inc=1, device_id=(peer, t, s), device_id_type=MESH)
    pl.semaphore_wait(barrier, n * n)

    pieces = [(w, u) for w in range(2) for u in range(SUB)]

    def move(src, dst, send_sem, recv_sem, part_to, tp_to):
        return pltpu.make_async_remote_copy(
            src_ref=src,
            dst_ref=dst,
            send_sem=send_sem,
            recv_sem=recv_sem,
            device_id=(part_to, tp_to, s),
            device_id_type=MESH,
        )

    def start_if(copy, when):
        pl.when(when)(copy.start)
        sends.append((copy, when))

    above, below = t < n - 1, t > 0
    up, down = lax.rem(t + 1, n), lax.rem(t + n - 1, n)
    for c, (w, u) in enumerate(pieces):
        first = pl.multiple_of((part * SUB + u) * sub_rows, sub_rows)
        src = (kw_hbm, vw_hbm)[w].at[pl.ds(first, sub_rows), :]
        dst = wkv.at[t, w, part, u]
        start_if(move(src, dst, upsem.at[t, c], zsem.at[t, c], part, up), above)
        start_if(move(src, dst, dnsem.at[t, c], zsem.at[t, c], part, down), below)

    own_copies = [
        pltpu.make_async_copy(
            (kw_hbm, vw_hbm)[w].at[pl.ds((q * SUB + u) * sub_rows, sub_rows), :],
            wkv.at[t, w, q, u],
            lwsem.at[w, q, u],
        )
        for w in range(2)
        for q in range(2)
        for u in range(SUB)
    ]
    for copy in own_copies:
        copy.start()

    def mem_copies(i):
        return [
            pltpu.make_async_copy(
                mem_hbm.at[:, pl.ds(pl.multiple_of(i * block + k * half_block, half_block), half_block)],
                mem.at[2 * i + k],
                msem.at[i, k],
            )
            for k in range(2)
        ]

    for d in range(n):
        for copy in mem_copies(ring(t, d)):
            copy.start()

    def project(i, fresh):
        for copy in mem_copies(i):
            copy.wait()

        @pl.loop(0, mem.shape[1] // ROW_TILE)
        def _(j):
            at_rows = pl.ds(pl.multiple_of(j * ROW_TILE, ROW_TILE), ROW_TILE)
            for w in range(2):
                acc = jnp.zeros((ROW_TILE, kv * HD), jnp.float32) if fresh else acc_kv[w, at_rows, :]
                for k in range(2):
                    acc += jnp.dot(
                        mem[2 * i + k, at_rows, :],
                        wkv[i, w, k].reshape(half_block, kv * HD),
                        preferred_element_type=jnp.float32,
                    )
                acc_kv[w, at_rows, :] = acc

    def arrivals(d):
        yield ring(t, n - d), t - d >= 0, up, above, upsem
        yield ring(t, d), t + d < n, down, below, dnsem

    def relay(d):
        for c, (w, u) in enumerate(pieces):
            for i, here, onward, further, out_sem in arrivals(d):
                piece = wkv.at[i, w, part, u]

                @pl.when(here)
                def _():
                    move(piece, piece, out_sem.at[i, c], zsem.at[i, c], part, t).wait_recv()

                start_if(
                    move(piece, piece, out_sem.at[i, c], zsem.at[i, c], part, onward),
                    jnp.logical_and(here, further),
                )
                start_if(move(piece, piece, ysem.at[0, i, c], ysem.at[1, i, c], peer, t), here)

    def absorb(d):
        for i, here, _, _, _ in arrivals(d):

            @pl.when(here)
            def _():
                for c, (w, u) in enumerate(pieces):
                    piece = wkv.at[i, w, peer, u]
                    move(piece, piece, ysem.at[0, i, c], ysem.at[1, i, c], peer, t).wait_recv()
                project(i, False)

    def columns(i):
        return pl.ds(pl.multiple_of(i * block, block), block)

    for d in range(1, n):
        g = ring(s, d)
        send(hidden_ref.at[:, :, columns(g)], hb.at[s], hsem, g, s, t, g)
    hb[s] = hidden_ref[:, :, columns(s)]
    for copy in own_copies:
        copy.wait()
    project(t, True)
    for d in range(1, n):
        g = ring(s, d)
        receive(hb.at[g], hsem, g)
    for r in range(n):
        held = jnp.zeros((rows, block), jnp.float32)
        for g in range(n):
            for c in range(cap):
                chosen = map_ref[g, c * n + r] > 0
                held = jnp.where(chosen, hb[g, c].astype(jnp.float32), held)
        st[0, r] = held.astype(jnp.bfloat16)

    for step in range(STEPS):
        state = st[step].reshape(n * rows, block).astype(jnp.float32)
        xs[...] = (state * gain_ref[...]).astype(jnp.bfloat16)
        squares = jnp.sum(state * state, axis=-1, keepdims=True)
        sn[step] = jnp.broadcast_to(squares, (n * rows, HD)).reshape(n, rows, HD)
        for d in range(1, n):
            g = ring(s, d)
            send(sn.at[step].at[g], rn.at[step].at[s], nsem.at[step], g, s, t, g)
        if step == 0:
            qcopy.wait()

        @pl.loop(0, block // TILE)
        def _(j):
            at_cols = pl.ds(pl.multiple_of(j * TILE, TILE), TILE)
            acc = jnp.dot(xs[...], qw[:, at_cols], preferred_element_type=jnp.float32)
            sq[step, :, :, at_cols] = acc.astype(jnp.bfloat16).reshape(n, rows, TILE)

        for d in range(1, n):
            g = ring(s, d)
            send(sq.at[step].at[g], rq.at[step].at[s], qsem.at[step], g, s, t, g)
        if step == 0:
            relay(1)
        total = sq[step, s].astype(jnp.float32)
        norms = sn[step, s]
        for d in range(1, n):
            g = ring(s, d)
            receive(rn.at[step].at[g], nsem.at[step], g)
            receive(rq.at[step].at[g], qsem.at[step], g)
            total += rq[step, g].astype(jnp.float32)
            norms += rn[step, g]
        scale = lax.rsqrt(norms[:, :1] * (1.0 / width) + EPSILON)
        for h in range(block // HD):
            head = total[:, h * HD : (h + 1) * HD] * scale
            mean = jnp.mean(head * head, axis=-1, keepdims=True)
            qn[step, :, h * HD : (h + 1) * HD] = (
                head * lax.rsqrt(mean + EPSILON) * qgain_ref[...]
            ).astype(jnp.bfloat16)
        for d in range(1, n):
            send(qn.at[step], aq.at[step].at[s], asem.at[step], d, s, ring(t, d), t)
        send_or_keep(qn.at[step], aq.at[step].at[s], asem.at[step], 0, s, t, t)

        if step == 0:
            for d in range(2, n):
                absorb(d - 1)
                relay(d)
            absorb(n - 1)
            ocopies = [
                pltpu.make_async_copy(
                    ow_hbm.at[
                        pl.ds(k * half_block, half_block), pl.ds(c * half_block, half_block)
                    ],
                    mem.at[2 * k + c],
                    wsem.at[1 + 2 * k + c],
                )
                for c in range(2)
                for k in range(2)
            ]
            for copy in ocopies:
                copy.start()

            @pl.loop(0, n)
            def _(r):
                at_rows = pl.ds(pl.multiple_of(r * toks, toks), toks)
                for j in range(kv):
                    cols = slice(j * HD, (j + 1) * HD)
                    keys_ref[r, :, cols] = head_norm(acc_kv[0, at_rows, cols], kgain_ref[...]).astype(
                        jnp.bfloat16
                    )
                values_ref[r] = acc_kv[1, at_rows, :].astype(jnp.bfloat16)

        position = t * toks + lax.broadcasted_iota(jnp.int32, (1, toks), 1)
        lane = lax.broadcasted_iota(jnp.int32, (rows, HD), 1)
        for d in (1, 2, 3, 0) if n == 4 else range(n - 1, -1, -1):
            r = ring(s, d)
            if d:
                receive(aq.at[step].at[r], asem.at[step], r)
            else:
                receive_or_kept(aq.at[step].at[r], asem.at[step], r)
            live = position < lens_ref[r]
            sums = jnp.zeros((rows, HD), jnp.float32)
            for j in range(kv):
                cols = slice(j * HD, (j + 1) * HD)
                heads = [
                    aq[step, r, :, (j * GROUP + g) * HD : (j * GROUP + g + 1) * HD]
                    for g in range(GROUP)
                ]
                scores = lax.dot_general(
                    jnp.concatenate(heads, axis=0),
                    keys_ref[r, :, cols],
                    (((1,), (1,)), ((), ())),
                    preferred_element_type=jnp.float32,
                )
                raw = jnp.where(live, jnp.exp(scores), 0.0)
                total_raw = jnp.sum(raw, axis=-1, keepdims=True)
                mixed = jnp.dot(
                    raw.astype(jnp.bfloat16),
                    values_ref[r, :, cols],
                    preferred_element_type=jnp.float32,
                ).astype(jnp.bfloat16)
                for g in range(GROUP):
                    h = j * GROUP + g
                    span = slice(g * rows, (g + 1) * rows)
                    so[step, r, :, h * HD : (h + 1) * HD] = mixed[span]
                    sums = jnp.where(lane == h, total_raw[span], sums)
            sl[step, r] = sums
            if d:
                send(sl.at[step].at[r], xl.at[step].at[s], xlsem.at[step], r, s, t, r)
                send(so.at[step].at[r], xo.at[step].at[s], xosem.at[step], r, s, t, r)
        xl[step, s] = sl[step, s]
        xo[step, s] = so[step, s]
        for d in (1, 2, 3, 0) if n == 4 else range(n - 1, -1, -1):
            h = ring(s, d)
            if d:
                receive(xl.at[step].at[h], xlsem.at[step], h)
                receive(xo.at[step].at[h], xosem.at[step], h)
            away = h != t
            for src, dst, sems in ((xl, rl, lsem), (xo, ro, osem)):
                piece, slot = src.at[step].at[h], dst.at[step].at[t]
                start_if(remote(piece, slot, sems.at[step], h, t, h, s), away)
        rl[step, t] = xl[step, t]
        ro[step, t] = xo[step, t]
        for d in range(1, n):
            i = ring(t, d)
            receive(rl.at[step].at[i], lsem.at[step], i)
            receive(ro.at[step].at[i], osem.at[step], i)
        sums = rl[step, 0]
        for i in range(1, n):
            sums += rl[step, i]
        for h in range(block // HD):
            cols = slice(h * HD, (h + 1) * HD)
            mixed = ro[step, 0, :, cols].astype(jnp.float32)
            for i in range(1, n):
                mixed += ro[step, i, :, cols].astype(jnp.float32)
            at[step, :, cols] = (mixed / sums[:, h : h + 1]).astype(jnp.bfloat16)
        for d in range(1, n):
            g = ring(s, d)
            send(at.at[step], aa.at[step].at[s], gsem.at[step], g, s, t, g)
        aa[step, s] = at[step]
        if step == 0:
            for copy in ocopies:
                copy.wait()
        for d in range(1, n):
            g = ring(s, d)
            receive(aa.at[step].at[g], gsem.at[step], g)

        for c in range(2):

            @pl.loop(0, half_block // TILE)
            def _(j):
                in_cols = pl.ds(pl.multiple_of(j * TILE, TILE), TILE)
                at_cols = pl.ds(pl.multiple_of(c * half_block + j * TILE, TILE), TILE)
                mixed_rows = aa[step].reshape(n * rows, block)
                acc = jnp.dot(
                    mixed_rows[:, :half_block],
                    mem[c, :, in_cols],
                    preferred_element_type=jnp.float32,
                ) + jnp.dot(
                    mixed_rows[:, half_block:],
                    mem[2 + c, :, in_cols],
                    preferred_element_type=jnp.float32,
                )
                sb[step, :, :, at_cols] = acc.astype(jnp.bfloat16).reshape(n, rows, TILE)

            cols = slice(c * half_block, (c + 1) * half_block)
            for d in (2, 1, 3) if n == 4 else range(1, n):
                i = ring(t, d)
                send(
                    sb.at[step, i, :, cols],
                    rb.at[step, t, :, cols],
                    bsem.at[2 * step + c],
                    i,
                    t,
                    i,
                    s,
                )

        live_row = lax.broadcasted_iota(jnp.int32, (rows, 1), 0) < rows_ref[t]
        for c in range(2):
            cols = slice(c * half_block, (c + 1) * half_block)
            branch = sb[step, t, :, cols].astype(jnp.float32)
            for d in range(1, n):
                i = ring(t, d)
                receive(rb.at[step, i, :, cols], bsem.at[2 * step + c], i)
                branch += rb[step, i, :, cols].astype(jnp.float32)
            old = st[step, t, :, cols].astype(jnp.float32)
            st[step + 1, t, :, cols] = (old + jnp.where(live_row, branch, 0.0)).astype(jnp.bfloat16)
            for d in range(1, n):
                i = ring(t, d)
                own = st.at[step + 1, t, :, cols]
                send(own, own, ssem.at[2 * step + c], i, t, i, s)
        for c in range(2):
            cols = slice(c * half_block, (c + 1) * half_block)
            for d in range(1, n):
                i = ring(t, d)
                receive(st.at[step + 1, i, :, cols], ssem.at[2 * step + c], i)

    for d in (1, 2, 3, 0) if n == 4 else range(n - 1, -1, -1):
        g = ring(s, d)
        for c in range(cap):
            held = jnp.zeros((rows, block), jnp.float32)
            for r in range(n):
                chosen = map_ref[g, c * n + r] > 0
                held = jnp.where(chosen, st[STEPS, r].astype(jnp.float32), held)
            ob[g, c] = held.astype(jnp.bfloat16)
        if d:
            send(ob.at[g], rob.at[s], fsem, g, s, t, g)
    rob[s] = ob[s]
    for d in range(1, n):
        g = ring(s, d)
        receive(rob.at[g], fsem, g)
    for c in range(cap):
        occupied = map_ref[s, c * n] + map_ref[s, c * n + 1]
        for r in range(2, n):
            occupied += map_ref[s, c * n + r]
        for g in range(n):
            cols = slice(g * block, (g + 1) * block)
            out_ref[c, :, cols] = jnp.where(
                occupied > 0,
                rob[g, c].astype(jnp.float32),
                hidden_ref[c, :, cols].astype(jnp.float32),
            ).astype(jnp.bfloat16)
    for copy, when in sends:
        if when is None:
            copy.wait_send()
        else:
            pl.when(when)(copy.wait_send)


def decode(
    n,
    lens,
    row_counts,
    slot_map,
    hidden,
    gain,
    q_gain,
    k_gain,
    mem_rows,
    k_weight,
    v_weight,
    q_weight,
    o_weight,
):
    cap, rows, width = hidden.shape
    block = width // n
    feats = k_weight.shape[1]
    bf, f32 = jnp.bfloat16, jnp.float32
    vmem, smem = (pl.BlockSpec(memory_space=m) for m in (pltpu.VMEM, pltpu.SMEM))
    hbm = pl.BlockSpec(memory_space=pl.ANY)
    big, one = (STEPS, n, rows, block), (STEPS, rows, block)
    small = (STEPS, n, rows, HD)
    scratch = [
        pltpu.VMEM((2 * n, mem_rows.shape[0], block // 2), bf),
        pltpu.VMEM((n, 2, 2, SUB, block // 2 // SUB, feats), bf),
        pltpu.VMEM((2, mem_rows.shape[0], feats), f32),
        pltpu.VMEM((n, mem_rows.shape[0] // n, feats), bf),
        pltpu.VMEM((n, mem_rows.shape[0] // n, feats), bf),
        pltpu.VMEM(q_weight.shape, bf),
        pltpu.VMEM((n * rows, block), bf),
        pltpu.VMEM((n, cap, rows, block), bf),
        pltpu.VMEM((STEPS + 1, n, rows, block), bf),
        pltpu.VMEM(big, bf),
        pltpu.VMEM(big, bf),
        pltpu.VMEM(small, f32),
        pltpu.VMEM(small, f32),
        pltpu.VMEM(one, bf),
        pltpu.VMEM(big, bf),
        pltpu.VMEM(big, bf),
        pltpu.VMEM(big, bf),
        pltpu.VMEM(big, bf),
        pltpu.VMEM(small, f32),
        pltpu.VMEM(small, f32),
        pltpu.VMEM(small, f32),
        pltpu.VMEM(one, bf),
        pltpu.VMEM(big, bf),
        pltpu.VMEM(big, bf),
        pltpu.VMEM(big, bf),
        pltpu.VMEM((n, cap, rows, block), bf),
        pltpu.VMEM((n, cap, rows, block), bf),
        pltpu.SemaphoreType.DMA((5,)),
        pltpu.SemaphoreType.DMA((2, n)),
    ]
    scratch += [pltpu.SemaphoreType.DMA((STEPS, 2, n))] * 8
    scratch += [pltpu.SemaphoreType.DMA((2 * STEPS, 2, n))] * 2
    scratch += [
        pltpu.SemaphoreType.DMA((2, n)),
        pltpu.SemaphoreType.DMA((n, 2)),
        pltpu.SemaphoreType.DMA((2, 2, SUB)),
        pltpu.SemaphoreType.DMA((n, 2 * SUB)),
        pltpu.SemaphoreType.DMA((n, 2 * SUB)),
        pltpu.SemaphoreType.DMA((n, 2 * SUB)),
        pltpu.SemaphoreType.DMA((2, n, 2 * SUB)),
    ]
    return pl.pallas_call(
        functools.partial(decode_kernel, n),
        out_shape=jax.ShapeDtypeStruct(hidden.shape, bf),
        in_specs=[smem] * 3 + [vmem] * 4 + [hbm] * 5,
        out_specs=vmem,
        scratch_shapes=scratch,
        compiler_params=pltpu.CompilerParams(
            collective_id=0, has_side_effects=True, vmem_limit_bytes=VMEM_LIMIT
        ),
        name="decode",
    )(
        lens,
        row_counts,
        slot_map,
        hidden,
        gain,
        q_gain,
        k_gain,
        mem_rows,
        k_weight,
        v_weight,
        q_weight,
        o_weight,
    )


def square_body(
    memory,
    mem_lengths,
    decode_group,
    row_counts,
    hidden,
    norm_gain,
    q_weight,
    k_weight,
    v_weight,
    q_gain,
    k_gain,
    o_weight,
):
    n = lax.axis_size("tp")
    req_count, tok_local, model_width = memory.shape
    capacity = hidden.shape[0]
    mem_rows = memory.reshape(req_count * tok_local, model_width)
    slot_map = slot_onehot(decode_group, n, capacity).astype(jnp.int32)
    block = model_width // n
    gain = lax.dynamic_slice_in_dim(norm_gain, lax.axis_index("section") * block, block)
    return decode(
        n,
        mem_lengths,
        row_counts,
        slot_map.reshape(n, capacity * req_count),
        hidden,
        gain.astype(jnp.float32)[None, :],
        (q_gain * HD ** (-0.5))[None, :],
        k_gain[None, :],
        mem_rows,
        k_weight,
        v_weight,
        q_weight,
        o_weight,
    )


def body(
    memory,
    mem_lengths,
    decode_group,
    row_counts,
    hidden,
    norm_gain,
    q_weight,
    k_weight,
    v_weight,
    q_gain,
    k_gain,
    o_weight,
):
    tp_count = lax.axis_size("tp")
    section_count = lax.axis_size("section")
    req_count, tok_local, model_width = memory.shape
    capacity, row_count = (hidden.shape[0], hidden.shape[1])
    heads_local = q_weight.shape[1] // HD
    section_heads = k_weight.shape[1] // HD
    kv_local = max(1, heads_local // GROUP)
    per_kv = heads_local // kv_local
    mem_len = tok_local * tp_count
    mem_rows = memory.reshape(req_count * tok_local, model_width)
    key_acc = jnp.dot(
        mem_rows,
        lax.all_gather(k_weight, "tp", axis=0, tiled=True),
        preferred_element_type=jnp.float32,
    )
    value_acc = jnp.dot(
        mem_rows,
        lax.all_gather(v_weight, "tp", axis=0, tiled=True),
        preferred_element_type=jnp.float32,
    )
    key_heads = head_norm(key_acc.reshape(req_count, tok_local, section_heads, HD), k_gain).astype(
        jnp.bfloat16
    )
    value_heads = value_acc.reshape(req_count, tok_local, section_heads, HD).astype(jnp.bfloat16)
    packed = jnp.stack([key_heads, value_heads], axis=2)
    slot_map = slot_onehot(decode_group, section_count, capacity)
    outgoing = jnp.einsum(
        "gcr,rtvjd->gjctvd",
        slot_map.astype(jnp.bfloat16),
        packed,
        preferred_element_type=jnp.float32,
    ).astype(jnp.bfloat16)
    by_head = lax.all_to_all(outgoing, "section", split_axis=0, concat_axis=1, tiled=True)[0]
    repeat_count = tp_count * kv_local // KVH
    grouped = by_head.reshape(KVH // kv_local, kv_local, capacity, tok_local, 2, HD)
    spread = jnp.repeat(grouped, repeat_count, axis=0)
    mine = lax.all_to_all(spread, "tp", split_axis=0, concat_axis=3, tiled=True)[0]
    keys_mine = mine[:, :, :, 0, :]
    values_mine = mine[:, :, :, 1, :]
    q_full, o_full = (
        lax.all_gather(q_weight, "section", axis=0, tiled=True),
        lax.all_gather(o_weight, "section", axis=1, tiled=True),
    )
    group_index = lax.axis_index("section")
    my_slots = lax.dynamic_index_in_dim(slot_map, group_index, 0, keepdims=False)
    occupied = jnp.sum(my_slots, axis=1)
    key_len = (
        jnp.sum(my_slots * mem_lengths.astype(jnp.float32)[None, :], axis=1)
        + (1.0 - occupied) * mem_len
    )
    live_count = jnp.sum(my_slots * row_counts.astype(jnp.float32)[None, :], axis=1)
    key_mask = (jnp.arange(mem_len, dtype=jnp.float32)[None, :] < key_len[:, None]).astype(
        jnp.float32
    )
    row_live = (jnp.arange(row_count, dtype=jnp.float32)[None, :] < live_count[:, None]).astype(
        jnp.float32
    )
    state = hidden
    for step_index in range(STEPS):
        state_f32 = state.astype(jnp.float32)
        normed = (
            state_f32
            * lax.rsqrt(jnp.mean(state_f32 * state_f32, axis=-1, keepdims=True) + EPSILON)
            * norm_gain.astype(jnp.float32)
        ).astype(jnp.bfloat16)
        queries = jnp.dot(
            normed.reshape(capacity * row_count, model_width),
            q_full,
            preferred_element_type=jnp.float32,
        )
        queries = queries.reshape(capacity, row_count, kv_local, per_kv, HD)
        queries = (head_norm(queries, q_gain) * HD ** (-0.5)).astype(jnp.bfloat16)
        scores = jnp.einsum(
            "crkgd,kcld->crkgl", queries, keys_mine, preferred_element_type=jnp.float32
        )
        raw = jnp.exp(scores) * key_mask[:, None, None, None, :]
        softmax = (raw / jnp.sum(raw, axis=-1, keepdims=True)).astype(jnp.bfloat16)
        attended = jnp.einsum(
            "crkgl,kcld->crkgd", softmax, values_mine, preferred_element_type=jnp.float32
        )
        attended = attended.astype(jnp.bfloat16).reshape(capacity * row_count, heads_local * HD)
        branch = lax.psum(jnp.dot(attended, o_full, preferred_element_type=jnp.float32), "tp")
        state = (
            state_f32 + row_live[:, :, None] * branch.reshape(capacity, row_count, model_width)
        ).astype(jnp.bfloat16)
    return state


def solution(mesh):
    in_specs = (
        P("parts", "tp", None),
        P("parts"),
        P("parts"),
        P("parts"),
        P(("parts", "section"), None, None),
        P(),
        P("section", "tp"),
        P("tp", "section"),
        P("tp", "section"),
        P(),
        P(),
        P("tp", "section"),
    )
    out_specs = P(("parts", "section"), None, None)

    def whole(memory, *rest):
        parts, tp = mesh.shape["parts"], mesh.shape["tp"]
        requests, tokens, width = memory.shape
        square = parts == 2 and tp == mesh.shape["section"] and requests == parts * tp
        square = square and 2 * requests * tokens == parts * width
        form = square_body if square else body
        return jax.shard_map(
            form, mesh=mesh, in_specs=in_specs, out_specs=out_specs, check_vma=False
        )(memory, *rest)

    return whole
```

```python
import functools

import jax
import jax.numpy as jnp
from jax import lax
from jax.experimental import pallas as pl
from jax.experimental.pallas import tpu as pltpu
from jax.sharding import PartitionSpec as P

KVH = 8
HD = 128
STEPS = 2
GROUP = 8


EPSILON = 1e-06
MESH = pl.DeviceIdType.MESH
TILE = 512
VMEM_LIMIT = 60 * 1024 * 1024
SUB = 2
ROW_TILE = 256


def head_norm(values_in, gain_vector):
    return (
        values_in
        * lax.rsqrt(jnp.mean(values_in * values_in, axis=-1, keepdims=True) + EPSILON)
        * gain_vector
    )


def slot_onehot(decode_group, groups, capacity):
    total = decode_group.shape[0]
    ordinal = jnp.arange(total, dtype=jnp.int32)
    matches = decode_group[None, :] == decode_group[:, None]
    slot_rank = jnp.sum((matches & (ordinal[None, :] < ordinal[:, None])).astype(jnp.int32), axis=1)
    group_ids = jnp.arange(groups, dtype=jnp.int32)
    slot_ids = jnp.arange(capacity, dtype=jnp.int32)
    chosen = (decode_group[None, None, :] == group_ids[:, None, None]) & (
        slot_rank[None, None, :] == slot_ids[None, :, None]
    )
    return chosen.astype(jnp.float32)


def decode_kernel(
    n,
    lens_ref,
    rows_ref,
    map_ref,
    hidden_ref,
    gain_ref,
    qgain_ref,
    kgain_ref,
    mem_hbm,
    kw_hbm,
    vw_hbm,
    qw_hbm,
    ow_hbm,
    out_ref,
    mem,
    wkv,
    acc_kv,
    keys_ref,
    values_ref,
    qw,
    xs,
    hb,
    st,
    sq,
    rq,
    sn,
    rn,
    qn,
    aq,
    so,
    xo,
    ro,
    sl,
    xl,
    rl,
    at,
    aa,
    sb,
    rb,
    ob,
    rob,
    wsem,
    hsem,
    qsem,
    nsem,
    asem,
    xosem,
    xlsem,
    osem,
    lsem,
    gsem,
    bsem,
    ssem,
    fsem,
    msem,
    lwsem,
    upsem,
    dnsem,
    zsem,
    ysem,
):
    part = lax.axis_index("parts")
    t = lax.axis_index("tp")
    s = lax.axis_index("section")
    cap, rows, width = hidden_ref.shape
    block = width // n
    toks = keys_ref.shape[1]
    kv = keys_ref.shape[2] // HD
    peer = 1 - part
    sub_rows = wkv.shape[4]
    half_block = mem.shape[2]
    diag = s == t
    sends = []

    def remote(src, dst, sems, i_send, i_recv, tp, section):
        return pltpu.make_async_remote_copy(
            src_ref=src,
            dst_ref=dst,
            send_sem=sems.at[0].at[i_send],
            recv_sem=sems.at[1].at[i_recv],
            device_id=(part, tp, section),
            device_id_type=MESH,
        )

    def send(*args):
        copy = remote(*args)
        copy.start()
        sends.append((copy, None))

    def send_or_keep(src, dst, *args):
        copy = remote(src, dst, *args)

        @pl.when(diag)
        def _():
            dst[...] = src[...]

        @pl.when(jnp.logical_not(diag))
        def _():
            copy.start()

        sends.append((copy, jnp.logical_not(diag)))

    def receive(dst, sems, i):
        remote(dst, dst, sems, i, i, t, s).wait_recv()

    def receive_or_kept(dst, sems, i):
        @pl.when(jnp.logical_not(diag))
        def _():
            receive(dst, sems, i)

    def ring(me, d):
        return lax.rem(me + d, n)

    qcopy = pltpu.make_async_copy(qw_hbm, qw, wsem.at[0])
    qcopy.start()

    barrier = pltpu.get_barrier_semaphore()
    for dt in range(n):
        for ds in range(n):
            if dt or ds:
                pl.semaphore_signal(
                    barrier, inc=1, device_id=(part, ring(t, dt), ring(s, ds)), device_id_type=MESH
                )
    pl.semaphore_signal(barrier, inc=1, device_id=(peer, t, s), device_id_type=MESH)
    pl.semaphore_wait(barrier, n * n)

    pieces = [(w, u) for w in range(2) for u in range(SUB)]

    def move(src, dst, send_sem, recv_sem, part_to, tp_to):
        return pltpu.make_async_remote_copy(
            src_ref=src,
            dst_ref=dst,
            send_sem=send_sem,
            recv_sem=recv_sem,
            device_id=(part_to, tp_to, s),
            device_id_type=MESH,
        )

    def start_if(copy, when):
        pl.when(when)(copy.start)
        sends.append((copy, when))

    above, below = t < n - 1, t > 0
    up, down = lax.rem(t + 1, n), lax.rem(t + n - 1, n)
    for c, (w, u) in enumerate(pieces):
        first = pl.multiple_of((part * SUB + u) * sub_rows, sub_rows)
        src = (kw_hbm, vw_hbm)[w].at[pl.ds(first, sub_rows), :]
        dst = wkv.at[t, w, part, u]
        start_if(move(src, dst, upsem.at[t, c], zsem.at[t, c], part, up), above)
        start_if(move(src, dst, dnsem.at[t, c], zsem.at[t, c], part, down), below)

    own_copies = [
        pltpu.make_async_copy(
            (kw_hbm, vw_hbm)[w].at[pl.ds((q * SUB + u) * sub_rows, sub_rows), :],
            wkv.at[t, w, q, u],
            lwsem.at[w, q, u],
        )
        for w in range(2)
        for q in range(2)
        for u in range(SUB)
    ]
    for copy in own_copies:
        copy.start()

    def mem_copies(i):
        return [
            pltpu.make_async_copy(
                mem_hbm.at[:, pl.ds(pl.multiple_of(i * block + k * half_block, half_block), half_block)],
                mem.at[2 * i + k],
                msem.at[i, k],
            )
            for k in range(2)
        ]

    for d in range(n):
        for copy in mem_copies(ring(t, d)):
            copy.start()

    def project(i, fresh):
        for copy in mem_copies(i):
            copy.wait()

        @pl.loop(0, mem.shape[1] // ROW_TILE)
        def _(j):
            at_rows = pl.ds(pl.multiple_of(j * ROW_TILE, ROW_TILE), ROW_TILE)
            for w in range(2):
                acc = jnp.zeros((ROW_TILE, kv * HD), jnp.float32) if fresh else acc_kv[w, at_rows, :]
                for k in range(2):
                    acc += jnp.dot(
                        mem[2 * i + k, at_rows, :],
                        wkv[i, w, k].reshape(half_block, kv * HD),
                        preferred_element_type=jnp.float32,
                    )
                acc_kv[w, at_rows, :] = acc

    def arrivals(d):
        yield ring(t, n - d), t - d >= 0, up, above, upsem
        yield ring(t, d), t + d < n, down, below, dnsem

    def relay(d):
        for c, (w, u) in enumerate(pieces):
            for i, here, onward, further, out_sem in arrivals(d):
                piece = wkv.at[i, w, part, u]

                @pl.when(here)
                def _():
                    move(piece, piece, out_sem.at[i, c], zsem.at[i, c], part, t).wait_recv()

                start_if(
                    move(piece, piece, out_sem.at[i, c], zsem.at[i, c], part, onward),
                    jnp.logical_and(here, further),
                )
                start_if(move(piece, piece, ysem.at[0, i, c], ysem.at[1, i, c], peer, t), here)

    def absorb(d):
        for i, here, _, _, _ in arrivals(d):

            @pl.when(here)
            def _():
                for c, (w, u) in enumerate(pieces):
                    piece = wkv.at[i, w, peer, u]
                    move(piece, piece, ysem.at[0, i, c], ysem.at[1, i, c], peer, t).wait_recv()
                project(i, False)

    def columns(i):
        return pl.ds(pl.multiple_of(i * block, block), block)

    for d in range(1, n):
        g = ring(s, d)
        send(hidden_ref.at[:, :, columns(g)], hb.at[s], hsem, g, s, t, g)
    hb[s] = hidden_ref[:, :, columns(s)]
    for copy in own_copies:
        copy.wait()
    project(t, True)
    for d in range(1, n):
        g = ring(s, d)
        receive(hb.at[g], hsem, g)
    for r in range(n):
        held = jnp.zeros((rows, block), jnp.float32)
        for g in range(n):
            for c in range(cap):
                chosen = map_ref[g, c * n + r] > 0
                held = jnp.where(chosen, hb[g, c].astype(jnp.float32), held)
        st[0, r] = held.astype(jnp.bfloat16)

    for step in range(STEPS):
        state = st[step].reshape(n * rows, block).astype(jnp.float32)
        xs[...] = (state * gain_ref[...]).astype(jnp.bfloat16)
        squares = jnp.sum(state * state, axis=-1, keepdims=True)
        sn[step] = jnp.broadcast_to(squares, (n * rows, HD)).reshape(n, rows, HD)
        for d in range(1, n):
            g = ring(s, d)
            send(sn.at[step].at[g], rn.at[step].at[s], nsem.at[step], g, s, t, g)
        if step == 0:
            qcopy.wait()

        @pl.loop(0, block // TILE)
        def _(j):
            at_cols = pl.ds(pl.multiple_of(j * TILE, TILE), TILE)
            acc = jnp.dot(xs[...], qw[:, at_cols], preferred_element_type=jnp.float32)
            sq[step, :, :, at_cols] = acc.astype(jnp.bfloat16).reshape(n, rows, TILE)

        for d in range(1, n):
            g = ring(s, d)
            send(sq.at[step].at[g], rq.at[step].at[s], qsem.at[step], g, s, t, g)
        if step == 0:
            relay(1)
        total = sq[step, s].astype(jnp.float32)
        norms = sn[step, s]
        for d in range(1, n):
            g = ring(s, d)
            receive(rn.at[step].at[g], nsem.at[step], g)
            receive(rq.at[step].at[g], qsem.at[step], g)
            total += rq[step, g].astype(jnp.float32)
            norms += rn[step, g]
        scale = lax.rsqrt(norms[:, :1] * (1.0 / width) + EPSILON)
        for h in range(block // HD):
            head = total[:, h * HD : (h + 1) * HD] * scale
            mean = jnp.mean(head * head, axis=-1, keepdims=True)
            qn[step, :, h * HD : (h + 1) * HD] = (
                head * lax.rsqrt(mean + EPSILON) * qgain_ref[...]
            ).astype(jnp.bfloat16)
        for d in range(1, n):
            send(qn.at[step], aq.at[step].at[s], asem.at[step], d, s, ring(t, d), t)
        send_or_keep(qn.at[step], aq.at[step].at[s], asem.at[step], 0, s, t, t)

        if step == 0:
            for d in range(2, n):
                relay(d)
                absorb(d - 1)
            absorb(n - 1)
            ocopies = [
                pltpu.make_async_copy(
                    ow_hbm.at[
                        pl.ds(k * half_block, half_block), pl.ds(c * half_block, half_block)
                    ],
                    mem.at[2 * k + c],
                    wsem.at[1 + 2 * k + c],
                )
                for c in range(2)
                for k in range(2)
            ]
            for copy in ocopies:
                copy.start()

            @pl.loop(0, n)
            def _(r):
                at_rows = pl.ds(pl.multiple_of(r * toks, toks), toks)
                for j in range(kv):
                    cols = slice(j * HD, (j + 1) * HD)
                    keys_ref[r, :, cols] = head_norm(acc_kv[0, at_rows, cols], kgain_ref[...]).astype(
                        jnp.bfloat16
                    )
                values_ref[r] = acc_kv[1, at_rows, :].astype(jnp.bfloat16)

        position = t * toks + lax.broadcasted_iota(jnp.int32, (1, toks), 1)
        lane = lax.broadcasted_iota(jnp.int32, (rows, HD), 1)
        for d in (1, 2, 3, 0) if n == 4 else range(n - 1, -1, -1):
            r = ring(s, d)
            if d:
                receive(aq.at[step].at[r], asem.at[step], r)
            else:
                receive_or_kept(aq.at[step].at[r], asem.at[step], r)
            live = position < lens_ref[r]
            sums = jnp.zeros((rows, HD), jnp.float32)
            for j in range(kv):
                cols = slice(j * HD, (j + 1) * HD)
                heads = [
                    aq[step, r, :, (j * GROUP + g) * HD : (j * GROUP + g + 1) * HD]
                    for g in range(GROUP)
                ]
                scores = lax.dot_general(
                    jnp.concatenate(heads, axis=0),
                    keys_ref[r, :, cols],
                    (((1,), (1,)), ((), ())),
                    preferred_element_type=jnp.float32,
                )
                raw = jnp.where(live, jnp.exp(scores), 0.0)
                total_raw = jnp.sum(raw, axis=-1, keepdims=True)
                mixed = jnp.dot(
                    raw.astype(jnp.bfloat16),
                    values_ref[r, :, cols],
                    preferred_element_type=jnp.float32,
                ).astype(jnp.bfloat16)
                for g in range(GROUP):
                    h = j * GROUP + g
                    span = slice(g * rows, (g + 1) * rows)
                    so[step, r, :, h * HD : (h + 1) * HD] = mixed[span]
                    sums = jnp.where(lane == h, total_raw[span], sums)
            sl[step, r] = sums
            if d:
                send(sl.at[step].at[r], xl.at[step].at[s], xlsem.at[step], r, s, t, r)
                send(so.at[step].at[r], xo.at[step].at[s], xosem.at[step], r, s, t, r)
        xl[step, s] = sl[step, s]
        xo[step, s] = so[step, s]
        for d in (1, 2, 3, 0) if n == 4 else range(n - 1, -1, -1):
            h = ring(s, d)
            if d:
                receive(xl.at[step].at[h], xlsem.at[step], h)
                receive(xo.at[step].at[h], xosem.at[step], h)
            away = h != t
            for src, dst, sems in ((xl, rl, lsem), (xo, ro, osem)):
                piece, slot = src.at[step].at[h], dst.at[step].at[t]
                start_if(remote(piece, slot, sems.at[step], h, t, h, s), away)
        rl[step, t] = xl[step, t]
        ro[step, t] = xo[step, t]
        for d in range(1, n):
            i = ring(t, d)
            receive(rl.at[step].at[i], lsem.at[step], i)
            receive(ro.at[step].at[i], osem.at[step], i)
        sums = rl[step, 0]
        for i in range(1, n):
            sums += rl[step, i]
        for h in range(block // HD):
            cols = slice(h * HD, (h + 1) * HD)
            mixed = ro[step, 0, :, cols].astype(jnp.float32)
            for i in range(1, n):
                mixed += ro[step, i, :, cols].astype(jnp.float32)
            at[step, :, cols] = (mixed / sums[:, h : h + 1]).astype(jnp.bfloat16)
        for d in range(1, n):
            g = ring(s, d)
            send(at.at[step], aa.at[step].at[s], gsem.at[step], g, s, t, g)
        aa[step, s] = at[step]
        if step == 0:
            for copy in ocopies:
                copy.wait()
        for d in range(1, n):
            g = ring(s, d)
            receive(aa.at[step].at[g], gsem.at[step], g)

        for c in range(2):

            @pl.loop(0, half_block // TILE)
            def _(j):
                in_cols = pl.ds(pl.multiple_of(j * TILE, TILE), TILE)
                at_cols = pl.ds(pl.multiple_of(c * half_block + j * TILE, TILE), TILE)
                mixed_rows = aa[step].reshape(n * rows, block)
                acc = jnp.dot(
                    mixed_rows[:, :half_block],
                    mem[c, :, in_cols],
                    preferred_element_type=jnp.float32,
                ) + jnp.dot(
                    mixed_rows[:, half_block:],
                    mem[2 + c, :, in_cols],
                    preferred_element_type=jnp.float32,
                )
                sb[step, :, :, at_cols] = acc.astype(jnp.bfloat16).reshape(n, rows, TILE)

            cols = slice(c * half_block, (c + 1) * half_block)
            for d in (2, 1, 3) if n == 4 else range(1, n):
                i = ring(t, d)
                send(
                    sb.at[step, i, :, cols],
                    rb.at[step, t, :, cols],
                    bsem.at[2 * step + c],
                    i,
                    t,
                    i,
                    s,
                )

        live_row = lax.broadcasted_iota(jnp.int32, (rows, 1), 0) < rows_ref[t]
        for c in range(2):
            cols = slice(c * half_block, (c + 1) * half_block)
            branch = sb[step, t, :, cols].astype(jnp.float32)
            for d in range(1, n):
                i = ring(t, d)
                receive(rb.at[step, i, :, cols], bsem.at[2 * step + c], i)
                branch += rb[step, i, :, cols].astype(jnp.float32)
            old = st[step, t, :, cols].astype(jnp.float32)
            st[step + 1, t, :, cols] = (old + jnp.where(live_row, branch, 0.0)).astype(jnp.bfloat16)
            for d in range(1, n):
                i = ring(t, d)
                own = st.at[step + 1, t, :, cols]
                send(own, own, ssem.at[2 * step + c], i, t, i, s)
        for c in range(2):
            cols = slice(c * half_block, (c + 1) * half_block)
            for d in range(1, n):
                i = ring(t, d)
                receive(st.at[step + 1, i, :, cols], ssem.at[2 * step + c], i)

    for d in (1, 2, 3, 0) if n == 4 else range(n - 1, -1, -1):
        g = ring(s, d)
        for c in range(cap):
            held = jnp.zeros((rows, block), jnp.float32)
            for r in range(n):
                chosen = map_ref[g, c * n + r] > 0
                held = jnp.where(chosen, st[STEPS, r].astype(jnp.float32), held)
            ob[g, c] = held.astype(jnp.bfloat16)
        if d:
            send(ob.at[g], rob.at[s], fsem, g, s, t, g)
    rob[s] = ob[s]
    for d in range(1, n):
        g = ring(s, d)
        receive(rob.at[g], fsem, g)
    for c in range(cap):
        occupied = map_ref[s, c * n] + map_ref[s, c * n + 1]
        for r in range(2, n):
            occupied += map_ref[s, c * n + r]
        for g in range(n):
            cols = slice(g * block, (g + 1) * block)
            out_ref[c, :, cols] = jnp.where(
                occupied > 0,
                rob[g, c].astype(jnp.float32),
                hidden_ref[c, :, cols].astype(jnp.float32),
            ).astype(jnp.bfloat16)
    for copy, when in sends:
        if when is None:
            copy.wait_send()
        else:
            pl.when(when)(copy.wait_send)


def decode(
    n,
    lens,
    row_counts,
    slot_map,
    hidden,
    gain,
    q_gain,
    k_gain,
    mem_rows,
    k_weight,
    v_weight,
    q_weight,
    o_weight,
):
    cap, rows, width = hidden.shape
    block = width // n
    feats = k_weight.shape[1]
    bf, f32 = jnp.bfloat16, jnp.float32
    vmem, smem = (pl.BlockSpec(memory_space=m) for m in (pltpu.VMEM, pltpu.SMEM))
    hbm = pl.BlockSpec(memory_space=pl.ANY)
    big, one = (STEPS, n, rows, block), (STEPS, rows, block)
    small = (STEPS, n, rows, HD)
    scratch = [
        pltpu.VMEM((2 * n, mem_rows.shape[0], block // 2), bf),
        pltpu.VMEM((n, 2, 2, SUB, block // 2 // SUB, feats), bf),
        pltpu.VMEM((2, mem_rows.shape[0], feats), f32),
        pltpu.VMEM((n, mem_rows.shape[0] // n, feats), bf),
        pltpu.VMEM((n, mem_rows.shape[0] // n, feats), bf),
        pltpu.VMEM(q_weight.shape, bf),
        pltpu.VMEM((n * rows, block), bf),
        pltpu.VMEM((n, cap, rows, block), bf),
        pltpu.VMEM((STEPS + 1, n, rows, block), bf),
        pltpu.VMEM(big, bf),
        pltpu.VMEM(big, bf),
        pltpu.VMEM(small, f32),
        pltpu.VMEM(small, f32),
        pltpu.VMEM(one, bf),
        pltpu.VMEM(big, bf),
        pltpu.VMEM(big, bf),
        pltpu.VMEM(big, bf),
        pltpu.VMEM(big, bf),
        pltpu.VMEM(small, f32),
        pltpu.VMEM(small, f32),
        pltpu.VMEM(small, f32),
        pltpu.VMEM(one, bf),
        pltpu.VMEM(big, bf),
        pltpu.VMEM(big, bf),
        pltpu.VMEM(big, bf),
        pltpu.VMEM((n, cap, rows, block), bf),
        pltpu.VMEM((n, cap, rows, block), bf),
        pltpu.SemaphoreType.DMA((5,)),
        pltpu.SemaphoreType.DMA((2, n)),
    ]
    scratch += [pltpu.SemaphoreType.DMA((STEPS, 2, n))] * 8
    scratch += [pltpu.SemaphoreType.DMA((2 * STEPS, 2, n))] * 2
    scratch += [
        pltpu.SemaphoreType.DMA((2, n)),
        pltpu.SemaphoreType.DMA((n, 2)),
        pltpu.SemaphoreType.DMA((2, 2, SUB)),
        pltpu.SemaphoreType.DMA((n, 2 * SUB)),
        pltpu.SemaphoreType.DMA((n, 2 * SUB)),
        pltpu.SemaphoreType.DMA((n, 2 * SUB)),
        pltpu.SemaphoreType.DMA((2, n, 2 * SUB)),
    ]
    return pl.pallas_call(
        functools.partial(decode_kernel, n),
        out_shape=jax.ShapeDtypeStruct(hidden.shape, bf),
        in_specs=[smem] * 3 + [vmem] * 4 + [hbm] * 5,
        out_specs=vmem,
        scratch_shapes=scratch,
        compiler_params=pltpu.CompilerParams(
            collective_id=0, has_side_effects=True, vmem_limit_bytes=VMEM_LIMIT
        ),
        name="decode",
    )(
        lens,
        row_counts,
        slot_map,
        hidden,
        gain,
        q_gain,
        k_gain,
        mem_rows,
        k_weight,
        v_weight,
        q_weight,
        o_weight,
    )


def square_body(
    memory,
    mem_lengths,
    decode_group,
    row_counts,
    hidden,
    norm_gain,
    q_weight,
    k_weight,
    v_weight,
    q_gain,
    k_gain,
    o_weight,
):
    n = lax.axis_size("tp")
    req_count, tok_local, model_width = memory.shape
    capacity = hidden.shape[0]
    mem_rows = memory.reshape(req_count * tok_local, model_width)
    slot_map = slot_onehot(decode_group, n, capacity).astype(jnp.int32)
    block = model_width // n
    gain = lax.dynamic_slice_in_dim(norm_gain, lax.axis_index("section") * block, block)
    return decode(
        n,
        mem_lengths,
        row_counts,
        slot_map.reshape(n, capacity * req_count),
        hidden,
        gain.astype(jnp.float32)[None, :],
        (q_gain * HD ** (-0.5))[None, :],
        k_gain[None, :],
        mem_rows,
        k_weight,
        v_weight,
        q_weight,
        o_weight,
    )


def body(
    memory,
    mem_lengths,
    decode_group,
    row_counts,
    hidden,
    norm_gain,
    q_weight,
    k_weight,
    v_weight,
    q_gain,
    k_gain,
    o_weight,
):
    tp_count = lax.axis_size("tp")
    section_count = lax.axis_size("section")
    req_count, tok_local, model_width = memory.shape
    capacity, row_count = (hidden.shape[0], hidden.shape[1])
    heads_local = q_weight.shape[1] // HD
    section_heads = k_weight.shape[1] // HD
    kv_local = max(1, heads_local // GROUP)
    per_kv = heads_local // kv_local
    mem_len = tok_local * tp_count
    mem_rows = memory.reshape(req_count * tok_local, model_width)
    key_acc = jnp.dot(
        mem_rows,
        lax.all_gather(k_weight, "tp", axis=0, tiled=True),
        preferred_element_type=jnp.float32,
    )
    value_acc = jnp.dot(
        mem_rows,
        lax.all_gather(v_weight, "tp", axis=0, tiled=True),
        preferred_element_type=jnp.float32,
    )
    key_heads = head_norm(key_acc.reshape(req_count, tok_local, section_heads, HD), k_gain).astype(
        jnp.bfloat16
    )
    value_heads = value_acc.reshape(req_count, tok_local, section_heads, HD).astype(jnp.bfloat16)
    packed = jnp.stack([key_heads, value_heads], axis=2)
    slot_map = slot_onehot(decode_group, section_count, capacity)
    outgoing = jnp.einsum(
        "gcr,rtvjd->gjctvd",
        slot_map.astype(jnp.bfloat16),
        packed,
        preferred_element_type=jnp.float32,
    ).astype(jnp.bfloat16)
    by_head = lax.all_to_all(outgoing, "section", split_axis=0, concat_axis=1, tiled=True)[0]
    repeat_count = tp_count * kv_local // KVH
    grouped = by_head.reshape(KVH // kv_local, kv_local, capacity, tok_local, 2, HD)
    spread = jnp.repeat(grouped, repeat_count, axis=0)
    mine = lax.all_to_all(spread, "tp", split_axis=0, concat_axis=3, tiled=True)[0]
    keys_mine = mine[:, :, :, 0, :]
    values_mine = mine[:, :, :, 1, :]
    q_full, o_full = (
        lax.all_gather(q_weight, "section", axis=0, tiled=True),
        lax.all_gather(o_weight, "section", axis=1, tiled=True),
    )
    group_index = lax.axis_index("section")
    my_slots = lax.dynamic_index_in_dim(slot_map, group_index, 0, keepdims=False)
    occupied = jnp.sum(my_slots, axis=1)
    key_len = (
        jnp.sum(my_slots * mem_lengths.astype(jnp.float32)[None, :], axis=1)
        + (1.0 - occupied) * mem_len
    )
    live_count = jnp.sum(my_slots * row_counts.astype(jnp.float32)[None, :], axis=1)
    key_mask = (jnp.arange(mem_len, dtype=jnp.float32)[None, :] < key_len[:, None]).astype(
        jnp.float32
    )
    row_live = (jnp.arange(row_count, dtype=jnp.float32)[None, :] < live_count[:, None]).astype(
        jnp.float32
    )
    state = hidden
    for step_index in range(STEPS):
        state_f32 = state.astype(jnp.float32)
        normed = (
            state_f32
            * lax.rsqrt(jnp.mean(state_f32 * state_f32, axis=-1, keepdims=True) + EPSILON)
            * norm_gain.astype(jnp.float32)
        ).astype(jnp.bfloat16)
        queries = jnp.dot(
            normed.reshape(capacity * row_count, model_width),
            q_full,
            preferred_element_type=jnp.float32,
        )
        queries = queries.reshape(capacity, row_count, kv_local, per_kv, HD)
        queries = (head_norm(queries, q_gain) * HD ** (-0.5)).astype(jnp.bfloat16)
        scores = jnp.einsum(
            "crkgd,kcld->crkgl", queries, keys_mine, preferred_element_type=jnp.float32
        )
        raw = jnp.exp(scores) * key_mask[:, None, None, None, :]
        softmax = (raw / jnp.sum(raw, axis=-1, keepdims=True)).astype(jnp.bfloat16)
        attended = jnp.einsum(
            "crkgl,kcld->crkgd", softmax, values_mine, preferred_element_type=jnp.float32
        )
        attended = attended.astype(jnp.bfloat16).reshape(capacity * row_count, heads_local * HD)
        branch = lax.psum(jnp.dot(attended, o_full, preferred_element_type=jnp.float32), "tp")
        state = (
            state_f32 + row_live[:, :, None] * branch.reshape(capacity, row_count, model_width)
        ).astype(jnp.bfloat16)
    return state


def solution(mesh):
    in_specs = (
        P("parts", "tp", None),
        P("parts"),
        P("parts"),
        P("parts"),
        P(("parts", "section"), None, None),
        P(),
        P("section", "tp"),
        P("tp", "section"),
        P("tp", "section"),
        P(),
        P(),
        P("tp", "section"),
    )
    out_specs = P(("parts", "section"), None, None)

    def whole(memory, *rest):
        parts, tp = mesh.shape["parts"], mesh.shape["tp"]
        requests, tokens, width = memory.shape
        square = parts == 2 and tp == mesh.shape["section"] and requests == parts * tp
        square = square and 2 * requests * tokens == parts * width
        form = square_body if square else body
        return jax.shard_map(
            form, mesh=mesh, in_specs=in_specs, out_specs=out_specs, check_vma=False
        )(memory, *rest)

    return whole
```
